512 devices in a mesh: azi: 16 (over y_hi, x), ra: 32 (over y_lo, z, core).
Axes of the slice: x: 4, y: 8 (y_hi: 4, y_lo: 2; y = y_hi * 2 + y_lo), z: 8, core: 2. Of those that a mesh axis runs over, the one named last changes fastest.
Arguments:
- vorticity: float32 [3, 128, 512, 1024], P(None, 'azi', 'ra'), may hold values from -6 to 6
- rotor_field: bfloat16 [3, 128, 512, 1024], P(None, 'azi', 'ra'), may hold values from -6 to 6
- courant: bfloat16 [3, 128, 512, 1024], P(None, 'azi', 'ra'), may hold values from -0.44921875 to 0.44921875
- load_tiles: float32 [16, 32, 128, 384], P('azi', 'ra'), may hold values from -6 to 6
- tile_block: int32 [16, 32, 128], P('azi', 'ra'), may hold values from 0 to 1023
- tile_count: int32 [16, 32, 32], P('azi', 'ra'), may hold values from 0 to 4, as said below
Outputs:
- vorticity_next: float32 [3, 128, 512, 1024], P(None, 'azi', 'ra')
The draws below stay inside these ranges and needn't reach their ends.
Inputs may be any that keep to these rules, and one draw needn't show every extreme that they name: `tile_count`: in every azimuth group of devices one destination radial device receives 4 used slots from every source device; slots at or beyond the count are padding. `tile_block`: several tiles may name the same cell block.
All inputs are finite; a program needn't handle non-finite values.
Results may differ from the reference program's by a relative error of at most 0.0003.
Values may be sent and summed in bfloat16 or wider, within the bound.
A program may use at most 64 MiB of HBM per device.

```python
import jax
import jax.numpy as jnp
from jax import lax

CA = 8
CR = 16
CZ = 1024
TS = 128
CAP = 4
SLOTS = 128
NA = 128
NR = 512
NB = 1024
N_AZI = 16
N_RA = 32


def draw_tile_count(key, part):
    key_base, key_hot = jax.random.split(jax.random.fold_in(key, 11))
    base_count = jax.random.randint(key_base, (N_AZI, N_RA, N_RA), 0, CAP + 1)
    hot_dest = jax.random.randint(key_hot, (N_AZI, 1, 1), 0, N_RA)
    dest_index = lax.broadcasted_iota(jnp.int32, (N_AZI, N_RA, N_RA), 2)
    return jnp.where(dest_index == hot_dest, CAP, base_count).astype(jnp.int32)


def plant(values, own_key, least, top_value):
    extent = values.shape
    place = [jax.random.randint(jax.random.fold_in(own_key, axis), (), 0, extent[axis]) for axis in range(len(extent))]
    values = values.at[tuple(place)].set(least)
    longest = extent.index(max(extent))
    place[longest] = (place[longest] + 1) % extent[longest]
    return values.at[tuple(place)].set(top_value)


def shard_levels(rng, dims, pieces, low, largest):
    factor_of, own = 1.0, jax.random.fold_in(rng, 6)
    for position, shards_of in pieces:
        draws = jnp.exp(jax.random.uniform(jax.random.fold_in(own, position), (shards_of,), jnp.float32, low / len(pieces), largest / len(pieces)))
        factor_of = factor_of * jnp.repeat(draws, dims[position] // shards_of).reshape([-1 if axis == position else 1 for axis in range(len(dims))])
    return factor_of


def gaussian(stream_key, extent, scale, limit, shards=(), kind=jnp.bfloat16):
    values = jax.random.normal(stream_key, extent, jnp.float32) * scale
    if len(shards) > 0:
        values = shard_levels(stream_key, extent, shards, -0.22, 0.18) * values
    return jnp.clip(values, min=-limit, max=limit).astype(kind)


def setup_inputs(seed: int = 0) -> dict:
    splits = jax.random.split(jax.random.key(seed), 7)
    return {
        "vorticity": gaussian(splits[0], (3, NA, NR, CZ), 1.0, 6.0, ((1, 16), (2, 32)), jnp.float32),
        "rotor_field": gaussian(splits[1], (3, NA, NR, CZ), 1.0, 6.0, ((1, 16), (2, 32))),
        "courant": jnp.clip(jax.random.uniform(splits[2], (3, NA, NR, CZ), jnp.float32, -0.44921875, 0.44921875) * shard_levels(splits[2], (3, NA, NR, CZ), ((1, 16), (2, 32)), -0.4, 0.0), -0.44921875, 0.44921875).astype(jnp.bfloat16),
        "load_tiles": gaussian(splits[3], (N_AZI, N_RA, SLOTS, 3 * TS), 1.0, 6.0, ((0, 16), (1, 32)), jnp.float32),
        "tile_block": plant(jax.random.randint(splits[4], (N_AZI, N_RA, SLOTS), 0, NB), jax.random.fold_in(splits[4], 1), 0, NB - 1).astype(jnp.int32),
        "tile_count": draw_tile_count(jax.random.fold_in(splits[6], 71), 0),
    }


DIFFUSION = 0.15


def advance_cells(combined, next_az, prev_az, next_rad, prev_rad, next_ax, prev_ax, courant, inverse, source_term):
    velocity = courant.astype(jnp.float32)
    inverse_sq = inverse * inverse
    up_rad = next_rad - combined
    down_rad = combined - prev_rad
    up_az = next_az - combined
    down_az = combined - prev_az
    up_ax = next_ax - combined
    down_ax = combined - prev_ax
    laplace = (up_rad - down_rad) + 0.25 * inverse * (up_rad + down_rad)
    laplace = laplace + inverse_sq * (up_az - down_az) + (up_ax - down_ax)
    advect = 0.5 * (velocity[0] * (up_rad + down_rad) + velocity[1] * inverse * (up_az + down_az) + velocity[2] * (up_ax + down_ax))
    coupling_rad = -0.25 * inverse_sq * combined[0] - 0.5 * inverse_sq * (next_az[1] - prev_az[1])
    coupling_az = -0.25 * inverse_sq * combined[1] + 0.5 * inverse_sq * (next_az[0] - prev_az[0])
    coupling = jnp.stack([coupling_rad, coupling_az, jnp.zeros_like(combined[2])])
    increment = DIFFUSION * (laplace + coupling) - advect + source_term
    return combined + increment


def place_loads(load_tiles, tile_block, tile_count):
    per_block = CZ // TS
    slot_index = jnp.arange(SLOTS, dtype=jnp.int32)
    slot_rank = slot_index % CAP
    live_slot = slot_rank[None, None, :] < jnp.repeat(tile_count, CAP, axis=2)
    values = load_tiles.reshape(N_AZI, N_RA, SLOTS, 3, TS) * live_slot[:, :, :, None, None].astype(jnp.float32)
    values = jnp.moveaxis(values, 3, 0)
    shape_idx = (N_AZI, N_RA, SLOTS)
    sector = lax.broadcasted_iota(jnp.int32, shape_idx, 0)
    dest_shard = jnp.broadcast_to((slot_index // CAP)[None, None, :], shape_idx).astype(jnp.int32)
    az_local = (tile_block // (CR * per_block)).astype(jnp.int32)
    rad_local = ((tile_block // per_block) % CR).astype(jnp.int32)
    ax_block = (tile_block % per_block).astype(jnp.int32)
    placed_grid = jnp.zeros((3, N_AZI, CA, N_RA, CR, per_block, TS), jnp.float32)
    placed_grid = placed_grid.at[:, sector, az_local, dest_shard, rad_local, ax_block, :].add(values)
    return placed_grid.reshape(3, NA, NR, CZ)


def reference(vorticity, rotor_field, courant, load_tiles, tile_block, tile_count):
    turned = jnp.roll(rotor_field, CA, axis=1)
    combined = vorticity + turned.astype(jnp.float32)
    radius = 0.5 + (jnp.arange(NR, dtype=jnp.float32) + 0.5) / NR
    inverse = (1.0 / radius)[:, None]
    next_az = jnp.roll(combined, -1, axis=1)
    prev_az = jnp.roll(combined, 1, axis=1)
    pad_rad = jnp.pad(combined, ((0, 0), (0, 0), (1, 1), (0, 0)))
    pad_ax = jnp.pad(combined, ((0, 0), (0, 0), (0, 0), (1, 1)))
    source_term = place_loads(load_tiles, tile_block, tile_count)
    return advance_cells(combined, next_az, prev_az, pad_rad[:, :, 2:], pad_rad[:, :, :-2], pad_ax[:, :, :, 2:], pad_ax[:, :, :, :-2], courant, inverse, source_term)
```

```python
import functools

import jax
import jax.numpy as jnp
from jax import lax
from jax.experimental import pallas as pl
from jax.experimental.pallas import tpu as pltpu
from jax.sharding import PartitionSpec as P

TS = 128
DIFFUSION = 0.15
MESH = pl.DeviceIdType.MESH
CHIP_X = 4

AROUND = (3, 4)
THROUGH = (0, 1, 2, 6)
STRAIGHT = (7, 0, 1, 2, 6, 5)
ORDER = (7, 0, 1, 2, 3, 4, 6, 5)


def kernel(
    vort, rotor, cour, tiles, tile_id, tile_n, out,
    vbuf, cbuf, rin, own0, comb, obuf, src, vup,
    relay_a, relay_b, relay_p, edge_out, edge_in,
    tbuf, idbuf, cntbuf, sbuf, trecv, tsib, tmat,
    lsem, osem, r_send, r_recv, a_send, a_recv, b_send, b_recv, c_send,
    p_send, p_recv, q_send, h_send, h_recv, e_send, e_recv, t_send, t_recv,
):
    n_azi, n_ra = lax.axis_size("azi"), lax.axis_size("ra")
    n_y = n_azi // CHIP_X
    n_chip = n_ra // 2
    rows_az, rows_rad, cells_ax = vbuf.shape[1:]
    j, r = lax.axis_index("azi"), lax.axis_index("ra")
    x, y = j % CHIP_X, j // CHIP_X
    chip, core = r // 2, r % 2
    first, last = x == 0, x == CHIP_X - 1

    def at(xx, yy):
        return ((yy % n_y) * CHIP_X + xx % CHIP_X, r)

    following = ((j + 1) % n_azi, r)
    preceding = ((j + n_azi - 1) % n_azi, r)
    up_x, down_x = at(x + 1, y), at(x + 3, y)
    up_y, down_y = at(x, y + 1), at(x, y + n_y - 1)
    sibling = (j, chip * 2 + 1 - core)

    def local(ref, dst, k):
        return pltpu.make_async_copy(ref, dst, lsem.at[k])

    def row(ref, k):
        return ref.at[:, pl.ds(k, 1)]

    loads = [
        local(tiles.at[0, 0], tbuf, 0),
        local(tile_id.at[0], idbuf, 1),
        local(tile_n.at[0], cntbuf, 2),
        local(vort, vbuf, 3),
        local(row(rotor, 0), own0, 4),
        local(cour, cbuf, 5),
    ]
    for load in loads:
        load.start()

    bar = pltpu.get_barrier_semaphore()

    def greet(device):
        pl.semaphore_signal(bar, inc=1, device_id=device, device_id_type=MESH)

    greet(following)
    greet(preceding)
    greet(sibling)
    for d in range(1, n_chip):
        greet((j, ((chip + d) % n_chip) * 2 + core))
    pl.when(last)(lambda: greet(up_x))
    pl.when(first)(lambda: greet(down_x))
    pl.when(x == 2)(lambda: greet(at(1, y + 1)))
    pl.when(x == 1)(lambda: greet(at(2, y + n_y - 1)))

    @pl.when(first)
    def _():
        greet(up_y)
        greet(down_y)

    outer_low = jnp.logical_and(core == 0, r > 0)
    outer_high = jnp.logical_and(core == 1, r < n_ra - 1)
    pl.when(outer_low)(lambda: greet((j, r - 1)))
    pl.when(outer_high)(lambda: greet((j, r + 1)))

    loads[0].wait()
    loads[1].wait()
    loads[2].wait()
    slots = tbuf.shape[0]
    slot = lax.broadcasted_iota(jnp.int32, (slots, slots), 0)
    lane = lax.broadcasted_iota(jnp.int32, (slots, slots), 1)
    ids = jnp.broadcast_to(idbuf[...].astype(jnp.float32), (slots, slots))
    id_col = jnp.sum(jnp.where(slot == lane, ids, 0.0), axis=1, keepdims=True)
    capacity = slots // n_ra
    slot_n = lax.broadcasted_iota(jnp.int32, (slots, n_ra), 0)
    lane_n = lax.broadcasted_iota(jnp.int32, (slots, n_ra), 1)
    counts = jnp.broadcast_to(cntbuf[...].astype(jnp.float32), (slots, n_ra))
    count_col = jnp.sum(
        jnp.where(slot_n // capacity == lane_n, counts, 0.0), axis=1, keepdims=True
    )
    used = (slot % capacity).astype(jnp.float32) < count_col
    width = tbuf.shape[1]
    sbuf[:, :width] = tbuf[...]
    sbuf[:, width:] = jnp.where(used, id_col, -1.0)
    group = 2 * capacity
    trecv[pl.ds(chip, 1)] = sbuf[pl.ds(pl.multiple_of(chip * group, group), group)][None]

    others = 3 + (n_chip - 1) + 1 + 2 * first.astype(jnp.int32)
    others = others + outer_low.astype(jnp.int32) + outer_high.astype(jnp.int32)
    pl.semaphore_wait(bar, others)

    def remote(source, target, send, recv, device):
        return pltpu.make_async_remote_copy(
            src_ref=source, dst_ref=target, send_sem=send, recv_sem=recv,
            device_id=device, device_id_type=MESH,
        )

    def straight(k):
        return remote(row(rotor, k), row(rin, k), r_send.at[k], r_recv.at[k], following)

    def through(k):
        i = THROUGH.index(k)
        return remote(row(rotor, k), row(relay_p, i), r_send.at[k], p_recv.at[i], up_x)

    def through_on(k):
        i = THROUGH.index(k)
        return remote(row(relay_p, i), row(rin, k), q_send.at[i], r_recv.at[k], up_y)

    def around(k):
        i = AROUND.index(k)
        return remote(row(rotor, k), row(relay_a, i), a_send.at[i], a_recv.at[i], down_x)

    def around_on(k, device):
        i = AROUND.index(k)
        return remote(row(relay_a, i), row(relay_b, i), b_send.at[i], b_recv.at[i], device)

    def around_end(k):
        i = AROUND.index(k)
        return remote(row(relay_b, i), row(rin, k), c_send.at[i], r_recv.at[k], down_x)

    low_edge = remote(row(vort, 0), vup, h_send.at[0], h_recv.at[0], preceding)
    high_edge = remote(row(comb, rows_az), row(comb, 0), h_send.at[1], h_recv.at[1], following)

    def radial(k, side, device):
        return remote(
            edge_out.at[side, k], edge_in.at[side, k], e_send.at[side, k], e_recv.at[side, k], device
        )

    def tile_copy(d):
        to = (chip + d) % n_chip
        return remote(
            sbuf.at[pl.ds(pl.multiple_of(to * group, group), group)], trecv.at[chip],
            t_send.at[d], t_recv.at[d], (j, to * 2 + core),
        )

    exchange = remote(trecv, tsib, t_send.at[0], t_recv.at[0], sibling)
    has_low, has_high = r > 0, r < n_ra - 1

    def start_row(k):
        if k in THROUGH:
            pl.when(last)(lambda: through(k).start())
            pl.when(jnp.logical_not(last))(lambda: straight(k).start())
        else:
            straight(k).start()

    start_row(7)
    around(AROUND[0]).start()
    low_edge.start()
    start_row(0)
    around(AROUND[1]).start()
    for d in range(1, n_chip):
        tile_copy(d).start()
    for k in STRAIGHT[2:]:
        start_row(k)

    @pl.when(jnp.logical_not(has_low))
    def _():
        edge_in[0] = jnp.zeros_like(edge_in[0])

    @pl.when(jnp.logical_not(has_high))
    def _():
        edge_in[1] = jnp.zeros_like(edge_in[1])

    def take(k):
        straight(k).wait_recv()
        for c in range(3):
            value = vbuf[c, k] + rin[c, k].astype(jnp.float32)
            comb[c, k + 1] = value
            edge_out[0, k, c : c + 1] = value[rows_rad - 1 :]
            edge_out[1, k, c : c + 1] = value[:1]
        pl.when(has_high)(lambda: radial(k, 0, (j, r + 1)).start())
        pl.when(has_low)(lambda: radial(k, 1, (j, r - 1)).start())

    def relay_through(k):
        @pl.when(first)
        def _():
            through(k).wait_recv()
            through_on(k).start()

    def relay_first(k):
        around(k).wait_recv()
        pl.when(x == 2)(lambda: around_on(k, at(1, y + 1)).start())
        pl.when(x != 2)(lambda: around_on(k, down_x).start())

    def relay_second(k):
        around_on(k, down_x).wait_recv()
        around_end(k).start()

    axial = lax.broadcasted_iota(jnp.int32, (rows_rad, cells_ax), 1)
    radial_row = lax.broadcasted_iota(jnp.int32, (rows_rad, cells_ax), 0)
    position = (r * rows_rad + radial_row).astype(jnp.float32)
    inverse = 1.0 / (0.5 + (position + 0.5) / (rows_rad * n_ra))
    inverse_sq = inverse * inverse

    def stencil(k):
        v0 = cbuf[0, k].astype(jnp.float32)
        v1 = cbuf[1, k].astype(jnp.float32)
        v2 = cbuf[2, k].astype(jnp.float32)
        rad = (0.25 * DIFFUSION) * inverse - 0.5 * v0
        azi_even = DIFFUSION * inverse_sq
        azi_odd = 0.5 * v1 * inverse
        axi = 0.5 * v2
        middle = (1.0 - 4.0 * DIFFUSION) - (2.0 * DIFFUSION) * inverse_sq
        turn = (0.5 * DIFFUSION) * inverse_sq
        for c in range(3):
            f = comb[c, k + 1]
            nxt, prv = comb[c, k + 2], comb[c, k]
            up = pltpu.roll(f, rows_rad - 1, 0)
            up = jnp.where(radial_row == rows_rad - 1, edge_in[1, k, c : c + 1], up)
            down = pltpu.roll(f, 1, 0)
            down = jnp.where(radial_row == 0, edge_in[0, k, c : c + 1], down)
            right = jnp.where(axial == cells_ax - 1, 0.0, pltpu.roll(f, cells_ax - 1, 1))
            left = jnp.where(axial == 0, 0.0, pltpu.roll(f, 1, 1))
            total = middle * f + src[c, k]
            total = total + DIFFUSION * ((up + down) + (right + left))
            total = total + rad * (up - down) - axi * (right - left)
            total = total + azi_even * (nxt + prv) - azi_odd * (nxt - prv)
            if c == 0:
                total = total - (0.5 * turn) * f - turn * (comb[1, k + 2] - comb[1, k])
            elif c == 1:
                total = total - (0.5 * turn) * f + turn * (comb[0, k + 2] - comb[0, k])
            obuf[c, k] = total

    def finish(k):
        pl.when(has_low)(lambda: radial(k, 0, (j, r)).wait_recv())
        pl.when(has_high)(lambda: radial(k, 1, (j, r)).wait_recv())
        stencil(k)
        pltpu.make_async_copy(row(obuf, k), row(out, k), osem.at[k]).start()

    loads[3].wait()
    take(7)
    high_edge.start()
    relay_first(AROUND[0])
    relay_through(0)
    take(0)
    relay_first(AROUND[1])
    relay_through(1)
    for d in range(1, n_chip):
        tile_copy(d).wait_recv()
    exchange.start()
    relay_second(AROUND[0])
    take(1)
    relay_through(2)
    relay_second(AROUND[1])

    exchange.wait_recv()
    keep = (slot % group) // capacity == core
    halves = []
    for i, got in enumerate((trecv, tsib)):
        part = got[...].reshape(slots, width + slots)
        value = part[:, :width]
        top = value.astype(jnp.bfloat16)
        tmat[i * slots : (i + 1) * slots] = top
        tmat[(2 + i) * slots : (3 + i) * slots] = (value - top.astype(jnp.float32)).astype(
            jnp.bfloat16
        )
        halves.append(jnp.where(keep, part[:, width:], -1.0).T)
    blocks = jnp.concatenate(halves, axis=1)
    m = lax.broadcasted_iota(jnp.int32, blocks.shape, 0)
    per_row = cells_ax // TS
    local_block = (m % rows_rad) * per_row + m // rows_rad
    for a in range(rows_az):
        wanted = (local_block + a * rows_rad * per_row).astype(jnp.float32)
        hot = jnp.where(blocks == wanted, 1.0, 0.0).astype(jnp.bfloat16)
        placed = jnp.dot(
            jnp.concatenate([hot, hot], axis=1), tmat[...], preferred_element_type=jnp.float32
        )
        for b in range(per_row):
            for c in range(3):
                src[c, a, :, b * TS : (b + 1) * TS] = placed[
                    b * rows_rad : (b + 1) * rows_rad, c * TS : (c + 1) * TS
                ]

    loads[4].wait()
    loads[5].wait()
    low_edge.wait_recv()
    for c in range(3):
        comb[c, rows_az + 1] = vup[c, 0] + own0[c, 0].astype(jnp.float32)
    high_edge.wait_recv()
    finish(0)
    relay_through(6)
    take(2)
    finish(1)
    take(3)
    finish(2)
    take(4)
    finish(3)
    take(6)
    finish(7)
    take(5)
    finish(4)
    finish(6)
    finish(5)

    for k in STRAIGHT:
        straight(k).wait_send()
    for k in AROUND:
        around(k).wait_send()
        around_on(k, down_x).wait_send()
        around_end(k).wait_send()

    @pl.when(first)
    def _():
        for k in THROUGH:
            through_on(k).wait_send()

    low_edge.wait_send()
    high_edge.wait_send()
    for d in range(1, n_chip):
        tile_copy(d).wait_send()
    exchange.wait_send()
    for k in range(rows_az):
        pl.when(has_high)(lambda k=k: radial(k, 0, (j, r)).wait_send())
        pl.when(has_low)(lambda k=k: radial(k, 1, (j, r)).wait_send())
        pltpu.make_async_copy(row(obuf, k), row(out, k), osem.at[k]).wait()


def body(vorticity, rotor_field, courant, load_tiles, tile_block, tile_count):
    shape = vorticity.shape
    _, rows_az, rows_rad, cells_ax = shape
    slots, width = load_tiles.shape[2:]
    n_ra = lax.axis_size("ra")
    n_chip = n_ra // 2
    group = slots // n_chip
    one_row = (3, 1, rows_rad, cells_ax)

    def relay(n):
        return pltpu.VMEM((3, n, rows_rad, cells_ax), jnp.bfloat16)

    dma = pltpu.SemaphoreType.DMA
    around, through = len(AROUND), len(THROUGH)
    scratch = [
        pltpu.VMEM(shape, jnp.float32),
        pltpu.VMEM(shape, jnp.bfloat16),
        pltpu.VMEM(shape, jnp.bfloat16),
        pltpu.VMEM(one_row, jnp.bfloat16),
        pltpu.VMEM((3, rows_az + 2, rows_rad, cells_ax), jnp.float32),
        pltpu.VMEM(shape, jnp.float32),
        pltpu.VMEM(shape, jnp.float32),
        pltpu.VMEM(one_row, jnp.float32),
        relay(around),
        relay(around),
        relay(through),
        pltpu.VMEM((2, rows_az, 3, cells_ax), jnp.float32),
        pltpu.VMEM((2, rows_az, 3, cells_ax), jnp.float32),
        pltpu.VMEM((slots, width), jnp.float32),
        pltpu.VMEM((1, slots), jnp.int32),
        pltpu.VMEM((1, n_ra), jnp.int32),
        pltpu.VMEM((slots, width + slots), jnp.float32),
        pltpu.VMEM((n_chip, group, width + slots), jnp.float32),
        pltpu.VMEM((n_chip, group, width + slots), jnp.float32),
        pltpu.VMEM((4 * slots, width), jnp.bfloat16),
        dma((6,)),
        dma((rows_az,)),
        dma((rows_az,)),
        dma((rows_az,)),
        dma((around,)),
        dma((around,)),
        dma((around,)),
        dma((around,)),
        dma((around,)),
        dma((through,)),
        dma((through,)),
        dma((through,)),
        dma((2,)),
        dma((2,)),
        dma((2, rows_az)),
        dma((2, rows_az)),
        dma((n_chip,)),
        dma((n_chip,)),
    ]
    return pl.pallas_call(
        kernel,
        name="step",
        out_shape=jax.ShapeDtypeStruct(shape, jnp.float32),
        in_specs=[pl.BlockSpec(memory_space=pltpu.HBM)] * 6,
        out_specs=pl.BlockSpec(memory_space=pl.ANY),
        scratch_shapes=scratch,
        compiler_params=pltpu.CompilerParams(
            collective_id=0, has_side_effects=True, vmem_limit_bytes=40 * 1024 * 1024
        ),
    )(vorticity, rotor_field, courant, load_tiles, tile_block, tile_count)


def solution(mesh):
    in_specs = (
        P(None, "azi", "ra", None),
        P(None, "azi", "ra", None),
        P(None, "azi", "ra", None),
        P("azi", "ra", None, None),
        P("azi", "ra", None),
        P("azi", "ra", None),
    )
    out_specs = P(None, "azi", "ra", None)
    return jax.shard_map(body, mesh=mesh, in_specs=in_specs, out_specs=out_specs, check_vma=False)
```

```python
import functools

import jax
import jax.numpy as jnp
from jax import lax
from jax.experimental import pallas as pl
from jax.experimental.pallas import tpu as pltpu
from jax.sharding import PartitionSpec as P

TS = 128
DIFFUSION = 0.15
MESH = pl.DeviceIdType.MESH
CHIP_X = 4

AROUND = (3, 4)
THROUGH = (0, 1, 2, 6, 5)
STRAIGHT = (7, 0, 1, 2, 6, 5)


def kernel(
    vort, rotor, cour, tiles, tile_id, tile_n, out,
    vbuf, cbuf, rbuf, rin, comb, obuf, src, vup,
    relay_a, relay_b, relay_p, edge_f, edge_s, edge_r, edge_out, edge_in,
    tbuf, idbuf, cntbuf, sbuf, trecv, tsib, tmat,
    lsem, osem, r_send, r_recv, a_send, a_recv, b_send, b_recv, c_send,
    p_recv, q_send, h_send, h_recv, e_send, e_recv, t_send, t_recv, up_sem, down_sem,
):
    n_azi, n_ra = lax.axis_size("azi"), lax.axis_size("ra")
    n_y = n_azi // CHIP_X
    n_chip = n_ra // 2
    n_z = n_chip // 2
    rows_az, rows_rad, cells_ax = vbuf.shape[1:]
    j, r = lax.axis_index("azi"), lax.axis_index("ra")
    x, y = j % CHIP_X, j // CHIP_X
    chip, core = r // 2, r % 2
    z = chip % n_z
    first, last = x == 0, x == CHIP_X - 1
    has_low, has_high = r > 0, r < n_ra - 1
    z_low, z_high = z > 0, z < n_z - 1
    near_low = jnp.logical_and(core == 0, z_low)
    near_high = jnp.logical_and(core == 1, z_high)
    seam_low = jnp.logical_and(jnp.logical_and(core == 0, z == 0), has_low)
    seam_high = jnp.logical_and(jnp.logical_and(core == 1, z == n_z - 1), has_high)

    def at(xx, yy):
        return ((yy % n_y) * CHIP_X + xx % CHIP_X, r)

    following = ((j + 1) % n_azi, r)
    preceding = ((j + n_azi - 1) % n_azi, r)
    up_x, down_x = at(x + 1, y), at(x + 3, y)
    up_y, down_y = at(x, y + 1), at(x, y + n_y - 1)
    sibling = (j, chip * 2 + 1 - core)
    above, below = (j, r + 2), (j, r - 2)
    lower, higher = (j, r - 1), (j, r + 1)

    def local(ref, dst, k):
        return pltpu.make_async_copy(ref, dst, lsem.at[k])

    def row(ref, k):
        return ref.at[:, pl.ds(k, 1)]

    loads = [
        local(rotor, rbuf, 0),
        local(vort, vbuf, 1),
        local(tiles.at[0, 0], tbuf, 2),
        local(tile_id.at[0], idbuf, 3),
        local(tile_n.at[0], cntbuf, 4),
        local(cour, cbuf, 5),
    ]
    for load in loads:
        load.start()

    bar = pltpu.get_barrier_semaphore()

    def greet(device):
        pl.semaphore_signal(bar, inc=1, device_id=device, device_id_type=MESH)

    greet(following)
    greet(preceding)
    greet(sibling)
    greet((j, (r + n_ra // 2) % n_ra))
    pl.when(last)(lambda: greet(up_x))
    pl.when(first)(lambda: greet(down_x))
    pl.when(x == 2)(lambda: greet(at(1, y + 1)))
    pl.when(x == 1)(lambda: greet(at(2, y + n_y - 1)))

    @pl.when(first)
    def _():
        greet(up_y)
        greet(down_y)

    pl.when(z_high)(lambda: greet(above))
    pl.when(z_low)(lambda: greet(below))
    pl.when(near_low)(lambda: greet(lower))
    pl.when(near_high)(lambda: greet(higher))
    others = 5 + 2 * first.astype(jnp.int32)
    for near in (z_high, z_low, near_low, near_high):
        others = others + near.astype(jnp.int32)

    loads[0].wait()
    for c in range(3):
        for k in range(rows_az):
            whole = rbuf[c, k].astype(jnp.float32)
            edge_f[c, k : k + 1] = whole[:1]
            edge_f[c, rows_az + k : rows_az + k + 1] = whole[rows_rad - 1 :]
    edge_s[...] = edge_f[...].astype(jnp.bfloat16)

    pl.semaphore_wait(bar, others)

    def remote(source, target, send, recv, device):
        return pltpu.make_async_remote_copy(
            src_ref=source, dst_ref=target, send_sem=send, recv_sem=recv,
            device_id=device, device_id_type=MESH,
        )

    def straight(k):
        return remote(row(rotor, k), row(rin, k), r_send.at[k], r_recv.at[k], following)

    def through(k):
        i = THROUGH.index(k)
        return remote(row(rotor, k), row(relay_p, i), r_send.at[k], p_recv.at[i], up_x)

    def through_on(k):
        i = THROUGH.index(k)
        return remote(row(relay_p, i), row(rin, k), q_send.at[i], r_recv.at[k], up_y)

    def around(k):
        i = AROUND.index(k)
        return remote(row(rotor, k), row(relay_a, i), a_send.at[i], a_recv.at[i], down_x)

    def around_on(k, device):
        i = AROUND.index(k)
        return remote(row(relay_a, i), row(relay_b, i), b_send.at[i], b_recv.at[i], device)

    def around_end(k):
        i = AROUND.index(k)
        return remote(row(relay_b, i), row(rin, k), c_send.at[i], r_recv.at[k], down_x)

    low_edge = remote(row(vort, 0), vup, h_send.at[0], h_recv.at[0], preceding)
    high_edge = remote(row(comb, rows_az), row(comb, 0), h_send.at[1], h_recv.at[1], following)
    edges = remote(edge_s, edge_r, h_send.at[2], h_recv.at[2], following)

    def radial(side, device):
        return remote(
            edge_out.at[side], edge_in.at[side], e_send.at[side], e_recv.at[side], device
        )

    capacity = tbuf.shape[0] // n_ra
    group = 2 * capacity

    def tile_copy(d):
        to = (chip + d) % n_chip
        return remote(
            sbuf.at[pl.ds(pl.multiple_of(to * group, group), group)], trecv.at[chip],
            t_send.at[d], t_recv.at[d], (j, to * 2 + core),
        )

    exchange = remote(trecv, tsib, t_send.at[0], t_recv.at[0], sibling)

    def start_row(k):
        if k in THROUGH:
            pl.when(last)(lambda: through(k).start())
            pl.when(jnp.logical_not(last))(lambda: straight(k).start())
        else:
            straight(k).start()

    start_row(7)
    around(AROUND[0]).start()
    edges.start()
    start_row(0)
    around(AROUND[1]).start()
    low_edge.start()
    for k in STRAIGHT[2:]:
        start_row(k)

    pl.when(z_low)(lambda: pl.semaphore_wait(up_sem, 1))
    pl.when(z_high)(
        lambda: pl.semaphore_signal(up_sem, inc=1, device_id=above, device_id_type=MESH)
    )

    loads[2].wait()
    loads[3].wait()
    loads[4].wait()
    slots = tbuf.shape[0]
    slot = lax.broadcasted_iota(jnp.int32, (slots, slots), 0)
    lane = lax.broadcasted_iota(jnp.int32, (slots, slots), 1)
    ids = jnp.broadcast_to(idbuf[...].astype(jnp.float32), (slots, slots))
    id_col = jnp.sum(jnp.where(slot == lane, ids, 0.0), axis=1, keepdims=True)
    slot_n = lax.broadcasted_iota(jnp.int32, (slots, n_ra), 0)
    lane_n = lax.broadcasted_iota(jnp.int32, (slots, n_ra), 1)
    counts = jnp.broadcast_to(cntbuf[...].astype(jnp.float32), (slots, n_ra))
    count_col = jnp.sum(
        jnp.where(slot_n // capacity == lane_n, counts, 0.0), axis=1, keepdims=True
    )
    used = (slot % capacity).astype(jnp.float32) < count_col
    width = tbuf.shape[1]
    sbuf[:, :width] = tbuf[...]
    sbuf[:, width:] = jnp.where(used, id_col, -1.0)
    trecv[pl.ds(chip, 1)] = sbuf[pl.ds(pl.multiple_of(chip * group, group), group)][None]

    def send_tiles(low_z, high_z):
        @pl.when(jnp.logical_and(z >= low_z, z <= high_z))
        def _():
            pl.when(z_high)(lambda: pl.semaphore_wait(down_sem, 1))
            pl.when(z_low)(
                lambda: pl.semaphore_signal(down_sem, inc=1, device_id=below, device_id_type=MESH)
            )
            for d in range(1, n_chip):
                tile_copy(d).start()

    def take(k):
        straight(k).wait_recv()
        for c in range(3):
            comb[c, k + 1] = vbuf[c, k] + rin[c, k].astype(jnp.float32)

    def relay_through(k):
        @pl.when(first)
        def _():
            through(k).wait_recv()
            through_on(k).start()

    def relay_first(k):
        around(k).wait_recv()
        pl.when(x == 2)(lambda: around_on(k, at(1, y + 1)).start())
        pl.when(x != 2)(lambda: around_on(k, down_x).start())

    def relay_second(k):
        around_on(k, down_x).wait_recv()
        around_end(k).start()

    send_tiles(n_z - 3, n_z - 1)
    loads[1].wait()
    for c in range(3):
        for k in range(rows_az):
            edge_out[1, c, k : k + 1] = vbuf[c, k, :1]
            edge_out[0, c, k : k + 1] = vbuf[c, k, rows_rad - 1 :]

    @pl.when(jnp.logical_not(has_low))
    def _():
        edge_in[0] = jnp.zeros_like(edge_in[0])

    @pl.when(jnp.logical_not(has_high))
    def _():
        edge_in[1] = jnp.zeros_like(edge_in[1])

    relay_first(AROUND[0])
    take(7)
    high_edge.start()
    relay_through(0)
    relay_first(AROUND[1])
    edges.wait_recv()
    for c in range(3):
        arrived = edge_r[c].astype(jnp.float32)
        edge_out[1, c] += arrived[:rows_az]
        edge_out[0, c] += arrived[rows_az:]
    in_run_low = jnp.logical_and(has_low, jnp.logical_not(seam_low))
    in_run_high = jnp.logical_and(has_high, jnp.logical_not(seam_high))
    pl.when(in_run_high)(lambda: radial(0, higher).start())
    pl.when(in_run_low)(lambda: radial(1, lower).start())
    send_tiles(3, n_z - 4)
    relay_second(AROUND[0])
    relay_through(1)
    take(0)
    relay_second(AROUND[1])
    relay_through(2)
    take(1)
    relay_through(6)
    send_tiles(0, 2)
    take(2)
    relay_through(5)
    for d in range(1, n_chip):
        tile_copy(d).wait_recv()
    exchange.start()
    pl.when(seam_high)(lambda: radial(0, higher).start())
    pl.when(seam_low)(lambda: radial(1, lower).start())

    axial = lax.broadcasted_iota(jnp.int32, (rows_rad, cells_ax), 1)
    radial_row = lax.broadcasted_iota(jnp.int32, (rows_rad, cells_ax), 0)
    position = (r * rows_rad + radial_row).astype(jnp.float32)
    inverse = 1.0 / (0.5 + (position + 0.5) / (rows_rad * n_ra))
    inverse_sq = inverse * inverse

    def stencil(k):
        v0 = cbuf[0, k].astype(jnp.float32)
        v1 = cbuf[1, k].astype(jnp.float32)
        v2 = cbuf[2, k].astype(jnp.float32)
        rad = (0.25 * DIFFUSION) * inverse - 0.5 * v0
        azi_even = DIFFUSION * inverse_sq
        azi_odd = 0.5 * v1 * inverse
        axi = 0.5 * v2
        middle = (1.0 - 4.0 * DIFFUSION) - (2.0 * DIFFUSION) * inverse_sq
        turn = (0.5 * DIFFUSION) * inverse_sq
        for c in range(3):
            f = comb[c, k + 1]
            nxt, prv = comb[c, k + 2], comb[c, k]
            up = pltpu.roll(f, rows_rad - 1, 0)
            up = jnp.where(radial_row == rows_rad - 1, edge_in[1, c, k : k + 1], up)
            down = pltpu.roll(f, 1, 0)
            down = jnp.where(radial_row == 0, edge_in[0, c, k : k + 1], down)
            right = jnp.where(axial == cells_ax - 1, 0.0, pltpu.roll(f, cells_ax - 1, 1))
            left = jnp.where(axial == 0, 0.0, pltpu.roll(f, 1, 1))
            total = middle * f + src[c, k]
            total = total + DIFFUSION * ((up + down) + (right + left))
            total = total + rad * (up - down) - axi * (right - left)
            total = total + azi_even * (nxt + prv) - azi_odd * (nxt - prv)
            if c == 0:
                total = total - (0.5 * turn) * f - turn * (comb[1, k + 2] - comb[1, k])
            elif c == 1:
                total = total - (0.5 * turn) * f + turn * (comb[0, k + 2] - comb[0, k])
            obuf[c, k] = total

    def finish(k):
        stencil(k)
        pltpu.make_async_copy(row(obuf, k), row(out, k), osem.at[k]).start()

    exchange.wait_recv()
    keep = (slot % group) // capacity == core
    halves = []
    for i, got in enumerate((trecv, tsib)):
        part = got[...].reshape(slots, width + slots)
        value = part[:, :width]
        top = value.astype(jnp.bfloat16)
        tmat[i * slots : (i + 1) * slots] = top
        tmat[(2 + i) * slots : (3 + i) * slots] = (value - top.astype(jnp.float32)).astype(
            jnp.bfloat16
        )
        halves.append(jnp.where(keep, part[:, width:], -1.0).T)
    blocks = jnp.concatenate(halves, axis=1)
    m = lax.broadcasted_iota(jnp.int32, blocks.shape, 0)
    per_row = cells_ax // TS
    local_block = (m % rows_rad) * per_row + m // rows_rad
    for a in range(rows_az):
        wanted = (local_block + a * rows_rad * per_row).astype(jnp.float32)
        hot = jnp.where(blocks == wanted, 1.0, 0.0).astype(jnp.bfloat16)
        placed = jnp.dot(
            jnp.concatenate([hot, hot], axis=1), tmat[...], preferred_element_type=jnp.float32
        )
        for b in range(per_row):
            for c in range(3):
                src[c, a, :, b * TS : (b + 1) * TS] = placed[
                    b * rows_rad : (b + 1) * rows_rad, c * TS : (c + 1) * TS
                ]

    loads[5].wait()
    low_edge.wait_recv()
    for c in range(3):
        comb[c, rows_az + 1] = vup[c, 0] + rbuf[c, 0].astype(jnp.float32)
    high_edge.wait_recv()
    pl.when(has_low)(lambda: radial(0, (j, r)).wait_recv())
    pl.when(has_high)(lambda: radial(1, (j, r)).wait_recv())
    finish(0)
    finish(1)
    take(3)
    finish(2)
    take(4)
    finish(3)
    take(6)
    finish(7)
    take(5)
    finish(4)
    finish(5)
    finish(6)

    for k in STRAIGHT:
        straight(k).wait_send()
    for k in AROUND:
        around(k).wait_send()
        around_on(k, down_x).wait_send()
        around_end(k).wait_send()

    @pl.when(first)
    def _():
        for k in THROUGH:
            through_on(k).wait_send()

    low_edge.wait_send()
    high_edge.wait_send()
    edges.wait_send()
    pl.when(has_high)(lambda: radial(0, (j, r)).wait_send())
    pl.when(has_low)(lambda: radial(1, (j, r)).wait_send())
    for d in range(1, n_chip):
        tile_copy(d).wait_send()
    exchange.wait_send()
    for k in range(rows_az):
        pltpu.make_async_copy(row(obuf, k), row(out, k), osem.at[k]).wait()


def body(vorticity, rotor_field, courant, load_tiles, tile_block, tile_count):
    shape = vorticity.shape
    _, rows_az, rows_rad, cells_ax = shape
    slots, width = load_tiles.shape[2:]
    n_ra = lax.axis_size("ra")
    n_chip = n_ra // 2
    group = slots // n_chip
    one_row = (3, 1, rows_rad, cells_ax)

    def relay(n):
        return pltpu.VMEM((3, n, rows_rad, cells_ax), jnp.bfloat16)

    dma = pltpu.SemaphoreType.DMA
    around, through = len(AROUND), len(THROUGH)
    scratch = [
        pltpu.VMEM(shape, jnp.float32),
        pltpu.VMEM(shape, jnp.bfloat16),
        pltpu.VMEM(shape, jnp.bfloat16),
        pltpu.VMEM(shape, jnp.bfloat16),
        pltpu.VMEM((3, rows_az + 2, rows_rad, cells_ax), jnp.float32),
        pltpu.VMEM(shape, jnp.float32),
        pltpu.VMEM(shape, jnp.float32),
        pltpu.VMEM(one_row, jnp.float32),
        relay(around),
        relay(around),
        relay(through),
        pltpu.VMEM((3, 2 * rows_az, cells_ax), jnp.float32),
        pltpu.VMEM((3, 2 * rows_az, cells_ax), jnp.bfloat16),
        pltpu.VMEM((3, 2 * rows_az, cells_ax), jnp.bfloat16),
        pltpu.VMEM((2, 3, rows_az, cells_ax), jnp.float32),
        pltpu.VMEM((2, 3, rows_az, cells_ax), jnp.float32),
        pltpu.VMEM((slots, width), jnp.float32),
        pltpu.VMEM((1, slots), jnp.int32),
        pltpu.VMEM((1, n_ra), jnp.int32),
        pltpu.VMEM((slots, width + slots), jnp.float32),
        pltpu.VMEM((n_chip, group, width + slots), jnp.float32),
        pltpu.VMEM((n_chip, group, width + slots), jnp.float32),
        pltpu.VMEM((4 * slots, width), jnp.bfloat16),
        dma((6,)),
        dma((rows_az,)),
        dma((rows_az,)),
        dma((rows_az,)),
        dma((around,)),
        dma((around,)),
        dma((around,)),
        dma((around,)),
        dma((around,)),
        dma((through,)),
        dma((through,)),
        dma((3,)),
        dma((3,)),
        dma((2,)),
        dma((2,)),
        dma((n_chip,)),
        dma((n_chip,)),
        pltpu.SemaphoreType.REGULAR,
        pltpu.SemaphoreType.REGULAR,
    ]
    return pl.pallas_call(
        kernel,
        name="step",
        out_shape=jax.ShapeDtypeStruct(shape, jnp.float32),
        in_specs=[pl.BlockSpec(memory_space=pltpu.HBM)] * 6,
        out_specs=pl.BlockSpec(memory_space=pl.ANY),
        scratch_shapes=scratch,
        compiler_params=pltpu.CompilerParams(
            collective_id=0, has_side_effects=True, vmem_limit_bytes=62 * 1024 * 1024
        ),
    )(vorticity, rotor_field, courant, load_tiles, tile_block, tile_count)


def solution(mesh):
    in_specs = (
        P(None, "azi", "ra", None),
        P(None, "azi", "ra", None),
        P(None, "azi", "ra", None),
        P("azi", "ra", None, None),
        P("azi", "ra", None),
        P("azi", "ra", None),
    )
    out_specs = P(None, "azi", "ra", None)
    return jax.shard_map(body, mesh=mesh, in_specs=in_specs, out_specs=out_specs, check_vma=False)
```

```python
import functools

import jax
import jax.numpy as jnp
from jax import lax
from jax.experimental import pallas as pl
from jax.experimental.pallas import tpu as pltpu
from jax.sharding import PartitionSpec as P

TS = 128
DIFFUSION = 0.15
MESH = pl.DeviceIdType.MESH
CHIP_X = 4

AROUND = (3, 4, 5)
AROUND_LAST = 5
THROUGH = (0, 1, 2, 6)
STRAIGHT = (0, 7, 5, 1, 2, 6)


def kernel(
    vort, rotor, cour, tiles, tile_id, tile_n, out,
    vbuf, cbuf, rbuf, rin, comb, src, vup,
    relay_a, relay_b, relay_p, edge_f, edge_s, edge_r, edge_out, edge_in,
    tbuf, idbuf, cntbuf, sbuf, trecv, tsib, tmat,
    lsem, r_send, r_recv, a_send, a_recv, b_send, b_recv, c_send,
    p_recv, q_send, h_send, h_recv, e_send, e_recv, t_send, t_recv, up_sem, down_sem,
):
    n_azi, n_ra = lax.axis_size("azi"), lax.axis_size("ra")
    n_y = n_azi // CHIP_X
    n_chip = n_ra // 2
    n_z = n_chip // 2
    rows_az, rows_rad, cells_ax = vbuf.shape[1:]
    j, r = lax.axis_index("azi"), lax.axis_index("ra")
    x, y = j % CHIP_X, j // CHIP_X
    chip, core = r // 2, r % 2
    z = chip % n_z
    first, last = x == 0, x == CHIP_X - 1
    has_low, has_high = r > 0, r < n_ra - 1
    z_low, z_high = z > 0, z < n_z - 1
    near_low = jnp.logical_and(core == 0, z_low)
    near_high = jnp.logical_and(core == 1, z_high)
    seam_low = jnp.logical_and(jnp.logical_and(core == 0, z == 0), has_low)
    seam_high = jnp.logical_and(jnp.logical_and(core == 1, z == n_z - 1), has_high)

    def at(xx, yy):
        return ((yy % n_y) * CHIP_X + xx % CHIP_X, r)

    following = ((j + 1) % n_azi, r)
    preceding = ((j + n_azi - 1) % n_azi, r)
    up_x, down_x = at(x + 1, y), at(x + 3, y)
    up_y, down_y = at(x, y + 1), at(x, y + n_y - 1)
    sibling = (j, chip * 2 + 1 - core)
    above, below = (j, r + 2), (j, r - 2)
    lower, higher = (j, r - 1), (j, r + 1)

    def local(ref, dst, k):
        return pltpu.make_async_copy(ref, dst, lsem.at[k])

    def row(ref, k):
        return ref.at[:, pl.ds(k, 1)]

    loads = [
        local(rotor, rbuf, 0),
        local(vort, vbuf, 1),
        local(tiles.at[0, 0], tbuf, 2),
        local(tile_id.at[0], idbuf, 3),
        local(tile_n.at[0], cntbuf, 4),
        local(cour, cbuf, 5),
    ]
    for load in loads:
        load.start()

    bar = pltpu.get_barrier_semaphore()

    def greet(device):
        pl.semaphore_signal(bar, inc=1, device_id=device, device_id_type=MESH)

    greet(following)
    greet(preceding)
    greet(sibling)
    greet((j, (r + n_ra // 2) % n_ra))
    pl.when(last)(lambda: greet(up_x))
    pl.when(first)(lambda: greet(down_x))
    pl.when(x == 2)(lambda: greet(at(1, y + 1)))
    pl.when(x == 1)(lambda: greet(at(2, y + n_y - 1)))

    @pl.when(first)
    def _():
        greet(up_y)
        greet(down_y)

    pl.when(z_high)(lambda: greet(above))
    pl.when(z_low)(lambda: greet(below))
    pl.when(near_low)(lambda: greet(lower))
    pl.when(near_high)(lambda: greet(higher))
    others = 5 + 2 * first.astype(jnp.int32)
    for near in (z_high, z_low, near_low, near_high):
        others = others + near.astype(jnp.int32)

    loads[0].wait()
    for c in range(3):
        for k in range(rows_az):
            whole = rbuf[c, k].astype(jnp.float32)
            edge_f[c, k : k + 1] = whole[:1]
            edge_f[c, rows_az + k : rows_az + k + 1] = whole[rows_rad - 1 :]
    edge_s[...] = edge_f[...].astype(jnp.bfloat16)

    pl.semaphore_wait(bar, others)

    def remote(source, target, send, recv, device):
        return pltpu.make_async_remote_copy(
            src_ref=source, dst_ref=target, send_sem=send, recv_sem=recv,
            device_id=device, device_id_type=MESH,
        )

    def straight(k):
        return remote(row(rotor, k), row(rin, k), r_send.at[k], r_recv.at[k], following)

    def through(k):
        i = THROUGH.index(k)
        return remote(row(rotor, k), row(relay_p, i), r_send.at[k], p_recv.at[i], up_x)

    def through_on(k):
        i = THROUGH.index(k)
        return remote(row(relay_p, i), row(rin, k), q_send.at[i], r_recv.at[k], up_y)

    def around(k):
        i = AROUND.index(k)
        return remote(row(rotor, k), row(relay_a, i), a_send.at[i], a_recv.at[i], down_x)

    def around_on(k, device):
        i = AROUND.index(k)
        return remote(row(relay_a, i), row(relay_b, i), b_send.at[i], b_recv.at[i], device)

    def around_end(k):
        i = AROUND.index(k)
        return remote(row(relay_b, i), row(rin, k), c_send.at[i], r_recv.at[k], down_x)

    low_edge = remote(row(vort, 0), vup, h_send.at[0], h_recv.at[0], preceding)
    high_edge = remote(row(comb, rows_az), row(comb, 0), h_send.at[1], h_recv.at[1], following)
    edges = remote(edge_s, edge_r, h_send.at[2], h_recv.at[2], following)

    def radial(side, device):
        return remote(
            edge_out.at[side], edge_in.at[side], e_send.at[side], e_recv.at[side], device
        )

    capacity = tbuf.shape[0] // n_ra
    group = 2 * capacity

    def tile_copy(d):
        to = (chip + d) % n_chip
        return remote(
            sbuf.at[pl.ds(pl.multiple_of(to * group, group), group)], trecv.at[chip],
            t_send.at[d], t_recv.at[d], (j, to * 2 + core),
        )

    exchange = remote(trecv, tsib, t_send.at[0], t_recv.at[0], sibling)

    def start_row(k):
        if k in THROUGH or k == AROUND_LAST:
            other_way = around if k == AROUND_LAST else through
            pl.when(last)(lambda: other_way(k).start())
            pl.when(jnp.logical_not(last))(lambda: straight(k).start())
        else:
            straight(k).start()

    start_row(0)
    start_row(7)
    around(3).start()
    start_row(5)
    edges.start()
    around(4).start()
    start_row(1)
    low_edge.start()
    start_row(2)
    start_row(6)

    pl.when(z_low)(lambda: pl.semaphore_wait(up_sem, 1))
    pl.when(z_high)(
        lambda: pl.semaphore_signal(up_sem, inc=1, device_id=above, device_id_type=MESH)
    )

    loads[2].wait()
    loads[3].wait()
    loads[4].wait()
    slots = tbuf.shape[0]
    slot = lax.broadcasted_iota(jnp.int32, (slots, slots), 0)
    lane = lax.broadcasted_iota(jnp.int32, (slots, slots), 1)
    ids = jnp.broadcast_to(idbuf[...].astype(jnp.float32), (slots, slots))
    id_col = jnp.sum(jnp.where(slot == lane, ids, 0.0), axis=1, keepdims=True)
    slot_n = lax.broadcasted_iota(jnp.int32, (slots, n_ra), 0)
    lane_n = lax.broadcasted_iota(jnp.int32, (slots, n_ra), 1)
    counts = jnp.broadcast_to(cntbuf[...].astype(jnp.float32), (slots, n_ra))
    count_col = jnp.sum(
        jnp.where(slot_n // capacity == lane_n, counts, 0.0), axis=1, keepdims=True
    )
    used = (slot % capacity).astype(jnp.float32) < count_col
    width = tbuf.shape[1]
    sbuf[:, :width] = tbuf[...]
    sbuf[:, width:] = jnp.where(used, id_col, -1.0)
    trecv[pl.ds(chip, 1)] = sbuf[pl.ds(pl.multiple_of(chip * group, group), group)][None]

    def send_tiles(low_z, high_z):
        @pl.when(jnp.logical_and(z >= low_z, z <= high_z))
        def _():
            pl.when(z_high)(lambda: pl.semaphore_wait(down_sem, 1))
            pl.when(z_low)(
                lambda: pl.semaphore_signal(down_sem, inc=1, device_id=below, device_id_type=MESH)
            )
            for d in range(1, n_chip):
                tile_copy(d).start()

    def take(k):
        straight(k).wait_recv()
        for c in range(3):
            comb[c, k + 1] = vbuf[c, k] + rin[c, k].astype(jnp.float32)

    def relay_through(k):
        @pl.when(first)
        def _():
            through(k).wait_recv()
            through_on(k).start()

    def relay_first(k):
        around(k).wait_recv()
        pl.when(x == 2)(lambda: around_on(k, at(1, y + 1)).start())
        pl.when(x != 2)(lambda: around_on(k, down_x).start())

    def relay_second(k):
        around_on(k, down_x).wait_recv()
        around_end(k).start()

    send_tiles(n_z - 2, n_z - 1)
    loads[1].wait()
    for c in range(3):
        for k in range(rows_az):
            edge_out[1, c, k : k + 1] = vbuf[c, k, :1]
            edge_out[0, c, k : k + 1] = vbuf[c, k, rows_rad - 1 :]

    @pl.when(jnp.logical_not(has_low))
    def _():
        edge_in[0] = jnp.zeros_like(edge_in[0])

    @pl.when(jnp.logical_not(has_high))
    def _():
        edge_in[1] = jnp.zeros_like(edge_in[1])

    relay_through(0)
    relay_first(3)
    take(7)
    high_edge.start()
    send_tiles(n_z - 3, n_z - 3)
    relay_through(1)
    pl.when(x == 2)(lambda: relay_first(5))
    relay_first(4)
    relay_through(2)
    edges.wait_recv()
    for c in range(3):
        arrived = edge_r[c].astype(jnp.float32)
        edge_out[1, c] += arrived[:rows_az]
        edge_out[0, c] += arrived[rows_az:]
    in_run_low = jnp.logical_and(has_low, jnp.logical_not(seam_low))
    in_run_high = jnp.logical_and(has_high, jnp.logical_not(seam_high))
    pl.when(in_run_high)(lambda: radial(0, higher).start())
    pl.when(in_run_low)(lambda: radial(1, lower).start())
    send_tiles(3, n_z - 4)
    relay_through(6)
    relay_second(3)
    pl.when(x == 1)(lambda: relay_second(5))
    relay_second(4)
    send_tiles(0, 2)
    take(0)
    take(1)
    take(5)

    @pl.when(seam_high)
    def _():
        tile_copy(n_chip - 1).wait_recv()
        radial(0, higher).start()

    @pl.when(seam_low)
    def _():
        tile_copy(1).wait_recv()
        radial(1, lower).start()

    pl.when(jnp.logical_not(seam_high))(lambda: tile_copy(n_chip - 1).wait_recv())
    pl.when(jnp.logical_not(seam_low))(lambda: tile_copy(1).wait_recv())
    for d in range(2, n_chip - 1):
        tile_copy(d).wait_recv()
    exchange.start()

    axial = lax.broadcasted_iota(jnp.int32, (rows_rad, cells_ax), 1)
    radial_row = lax.broadcasted_iota(jnp.int32, (rows_rad, cells_ax), 0)
    position = (r * rows_rad + radial_row).astype(jnp.float32)
    inverse = 1.0 / (0.5 + (position + 0.5) / (rows_rad * n_ra))
    inverse_sq = inverse * inverse

    def stencil(k):
        v0 = cbuf[0, k].astype(jnp.float32)
        v1 = cbuf[1, k].astype(jnp.float32)
        v2 = cbuf[2, k].astype(jnp.float32)
        rad = (0.25 * DIFFUSION) * inverse - 0.5 * v0
        azi_even = DIFFUSION * inverse_sq
        azi_odd = 0.5 * v1 * inverse
        axi = 0.5 * v2
        middle = (1.0 - 4.0 * DIFFUSION) - (2.0 * DIFFUSION) * inverse_sq
        turn = (0.5 * DIFFUSION) * inverse_sq
        for c in range(3):
            f = comb[c, k + 1]
            nxt, prv = comb[c, k + 2], comb[c, k]
            up = pltpu.roll(f, rows_rad - 1, 0)
            up = jnp.where(radial_row == rows_rad - 1, edge_in[1, c, k : k + 1], up)
            down = pltpu.roll(f, 1, 0)
            down = jnp.where(radial_row == 0, edge_in[0, c, k : k + 1], down)
            right = jnp.where(axial == cells_ax - 1, 0.0, pltpu.roll(f, cells_ax - 1, 1))
            left = jnp.where(axial == 0, 0.0, pltpu.roll(f, 1, 1))
            total = middle * f + src[c, k]
            total = total + DIFFUSION * ((up + down) + (right + left))
            total = total + rad * (up - down) - axi * (right - left)
            total = total + azi_even * (nxt + prv) - azi_odd * (nxt - prv)
            if c == 0:
                total = total - (0.5 * turn) * f - turn * (comb[1, k + 2] - comb[1, k])
            elif c == 1:
                total = total - (0.5 * turn) * f + turn * (comb[0, k + 2] - comb[0, k])
            out[c, k] = total

    exchange.wait_recv()
    keep = (slot % group) // capacity == core
    halves = []
    for i, got in enumerate((trecv, tsib)):
        part = got[...].reshape(slots, width + slots)
        value = part[:, :width]
        top = value.astype(jnp.bfloat16)
        tmat[i * slots : (i + 1) * slots] = top
        tmat[(2 + i) * slots : (3 + i) * slots] = (value - top.astype(jnp.float32)).astype(
            jnp.bfloat16
        )
        halves.append(jnp.where(keep, part[:, width:], -1.0).T)
    blocks = jnp.concatenate(halves, axis=1)
    m = lax.broadcasted_iota(jnp.int32, blocks.shape, 0)
    per_row = cells_ax // TS
    local_block = (m % rows_rad) * per_row + m // rows_rad
    for a in range(rows_az):
        wanted = (local_block + a * rows_rad * per_row).astype(jnp.float32)
        hot = jnp.where(blocks == wanted, 1.0, 0.0).astype(jnp.bfloat16)
        placed = jnp.dot(
            jnp.concatenate([hot, hot], axis=1), tmat[...], preferred_element_type=jnp.float32
        )
        for b in range(per_row):
            for c in range(3):
                src[c, a, :, b * TS : (b + 1) * TS] = placed[
                    b * rows_rad : (b + 1) * rows_rad, c * TS : (c + 1) * TS
                ]

    loads[5].wait()
    low_edge.wait_recv()
    for c in range(3):
        comb[c, rows_az + 1] = vup[c, 0] + rbuf[c, 0].astype(jnp.float32)
    high_edge.wait_recv()
    pl.when(has_low)(lambda: radial(0, (j, r)).wait_recv())
    pl.when(has_high)(lambda: radial(1, (j, r)).wait_recv())
    stencil(0)
    take(3)
    take(4)
    stencil(4)
    take(2)
    stencil(1)
    stencil(2)
    stencil(3)
    take(6)
    stencil(7)
    stencil(5)
    stencil(6)

    for k in STRAIGHT:
        if k != AROUND_LAST:
            straight(k).wait_send()
    for k in AROUND:
        if k != AROUND_LAST:
            around(k).wait_send()
            around_on(k, down_x).wait_send()
            around_end(k).wait_send()
    pl.when(last)(lambda: around(AROUND_LAST).wait_send())
    pl.when(jnp.logical_not(last))(lambda: straight(AROUND_LAST).wait_send())
    pl.when(x == 2)(lambda: around_on(AROUND_LAST, down_x).wait_send())
    pl.when(x == 1)(lambda: around_end(AROUND_LAST).wait_send())

    @pl.when(first)
    def _():
        for k in THROUGH:
            through_on(k).wait_send()

    low_edge.wait_send()
    high_edge.wait_send()
    edges.wait_send()
    pl.when(has_high)(lambda: radial(0, (j, r)).wait_send())
    pl.when(has_low)(lambda: radial(1, (j, r)).wait_send())
    for d in range(1, n_chip):
        tile_copy(d).wait_send()
    exchange.wait_send()


def body(vorticity, rotor_field, courant, load_tiles, tile_block, tile_count):
    shape = vorticity.shape
    _, rows_az, rows_rad, cells_ax = shape
    slots, width = load_tiles.shape[2:]
    n_ra = lax.axis_size("ra")
    n_chip = n_ra // 2
    group = slots // n_chip
    one_row = (3, 1, rows_rad, cells_ax)

    def relay(n):
        return pltpu.VMEM((3, n, rows_rad, cells_ax), jnp.bfloat16)

    dma = pltpu.SemaphoreType.DMA
    around, through = len(AROUND), len(THROUGH)
    scratch = [
        pltpu.VMEM(shape, jnp.float32),
        pltpu.VMEM(shape, jnp.bfloat16),
        pltpu.VMEM(shape, jnp.bfloat16),
        pltpu.VMEM(shape, jnp.bfloat16),
        pltpu.VMEM((3, rows_az + 2, rows_rad, cells_ax), jnp.float32),
        pltpu.VMEM(shape, jnp.float32),
        pltpu.VMEM(one_row, jnp.float32),
        relay(around),
        relay(around),
        relay(through),
        pltpu.VMEM((3, 2 * rows_az, cells_ax), jnp.float32),
        pltpu.VMEM((3, 2 * rows_az, cells_ax), jnp.bfloat16),
        pltpu.VMEM((3, 2 * rows_az, cells_ax), jnp.bfloat16),
        pltpu.VMEM((2, 3, rows_az, cells_ax), jnp.float32),
        pltpu.VMEM((2, 3, rows_az, cells_ax), jnp.float32),
        pltpu.VMEM((slots, width), jnp.float32),
        pltpu.VMEM((1, slots), jnp.int32),
        pltpu.VMEM((1, n_ra), jnp.int32),
        pltpu.VMEM((slots, width + slots), jnp.float32),
        pltpu.VMEM((n_chip, group, width + slots), jnp.float32),
        pltpu.VMEM((n_chip, group, width + slots), jnp.float32),
        pltpu.VMEM((4 * slots, width), jnp.bfloat16),
        dma((6,)),
        dma((rows_az,)),
        dma((rows_az,)),
        dma((around,)),
        dma((around,)),
        dma((around,)),
        dma((around,)),
        dma((around,)),
        dma((through,)),
        dma((through,)),
        dma((3,)),
        dma((3,)),
        dma((2,)),
        dma((2,)),
        dma((n_chip,)),
        dma((n_chip,)),
        pltpu.SemaphoreType.REGULAR,
        pltpu.SemaphoreType.REGULAR,
    ]
    return pl.pallas_call(
        kernel,
        name="step",
        out_shape=pltpu.VMEM(shape, jnp.float32),
        in_specs=[pl.BlockSpec(memory_space=pltpu.HBM)] * 6,
        out_specs=pl.BlockSpec(memory_space=pltpu.VMEM),
        scratch_shapes=scratch,
        compiler_params=pltpu.CompilerParams(
            collective_id=0, has_side_effects=True, vmem_limit_bytes=62 * 1024 * 1024
        ),
    )(vorticity, rotor_field, courant, load_tiles, tile_block, tile_count)


def solution(mesh):
    in_specs = (
        P(None, "azi", "ra", None),
        P(None, "azi", "ra", None),
        P(None, "azi", "ra", None),
        P("azi", "ra", None, None),
        P("azi", "ra", None),
        P("azi", "ra", None),
    )
    out_specs = P(None, "azi", "ra", None)
    return jax.shard_map(body, mesh=mesh, in_specs=in_specs, out_specs=out_specs, check_vma=False)
```

```python
import functools

import jax
import jax.numpy as jnp
from jax import lax
from jax.experimental import pallas as pl
from jax.experimental.pallas import tpu as pltpu
from jax.sharding import PartitionSpec as P

TS = 128
DIFFUSION = 0.15
MESH = pl.DeviceIdType.MESH
CHIP_X = 4

AROUND = (3, 4, 5)
AROUND_LAST = 5
THROUGH = (0, 1, 2, 6)
STRAIGHT = (0, 7, 5, 1, 2, 6)


def kernel(
    vort, rotor, cour, tiles, tile_id, tile_n, out,
    vbuf, cbuf, rbuf, rin, comb, src, vup,
    relay_a, relay_b, relay_p, edge_f, edge_s, edge_r, edge_out, edge_in,
    tbuf, idbuf, cntbuf, sbuf, trecv, tsib, tmat,
    lsem, r_send, r_recv, a_send, a_recv, b_send, b_recv, c_send,
    p_recv, q_send, h_send, h_recv, e_send, e_recv, t_send, t_recv, up_sem, down_sem, seam_sem,
):
    n_azi, n_ra = lax.axis_size("azi"), lax.axis_size("ra")
    n_y = n_azi // CHIP_X
    n_chip = n_ra // 2
    n_z = n_chip // 2
    rows_az, rows_rad, cells_ax = vbuf.shape[1:]
    j, r = lax.axis_index("azi"), lax.axis_index("ra")
    x, y = j % CHIP_X, j // CHIP_X
    chip, core = r // 2, r % 2
    z = chip % n_z
    first, last = x == 0, x == CHIP_X - 1
    has_low, has_high = r > 0, r < n_ra - 1
    z_low, z_high = z > 0, z < n_z - 1
    near_low = jnp.logical_and(core == 0, z_low)
    near_high = jnp.logical_and(core == 1, z_high)
    seam_low = jnp.logical_and(jnp.logical_and(core == 0, z == 0), has_low)
    seam_high = jnp.logical_and(jnp.logical_and(core == 1, z == n_z - 1), has_high)

    def at(xx, yy):
        return ((yy % n_y) * CHIP_X + xx % CHIP_X, r)

    following = ((j + 1) % n_azi, r)
    preceding = ((j + n_azi - 1) % n_azi, r)
    up_x, down_x = at(x + 1, y), at(x + 3, y)
    up_y, down_y = at(x, y + 1), at(x, y + n_y - 1)
    sibling = (j, chip * 2 + 1 - core)
    above, below = (j, r + 2), (j, r - 2)
    lower, higher = (j, r - 1), (j, r + 1)

    def local(ref, dst, k):
        return pltpu.make_async_copy(ref, dst, lsem.at[k])

    def row(ref, k):
        return ref.at[:, pl.ds(k, 1)]

    loads = [
        local(rotor, rbuf, 0),
        local(vort, vbuf, 1),
        local(tiles.at[0, 0], tbuf, 2),
        local(tile_id.at[0], idbuf, 3),
        local(tile_n.at[0], cntbuf, 4),
        local(cour, cbuf, 5),
    ]
    for load in loads:
        load.start()

    bar = pltpu.get_barrier_semaphore()

    def greet(device):
        pl.semaphore_signal(bar, inc=1, device_id=device, device_id_type=MESH)

    greet(following)
    greet(preceding)
    greet(sibling)
    greet((j, (r + n_ra // 2) % n_ra))
    pl.when(last)(lambda: greet(up_x))
    pl.when(first)(lambda: greet(down_x))
    pl.when(x == 2)(lambda: greet(at(1, y + 1)))
    pl.when(x == 1)(lambda: greet(at(2, y + n_y - 1)))
    pl.when(x == 1)(lambda: greet(at(0, y + 1)))

    @pl.when(first)
    def _():
        greet(up_y)
        greet(down_y)
        greet(at(1, y + n_y - 1))

    pl.when(z_high)(lambda: greet(above))
    pl.when(z_low)(lambda: greet(below))
    pl.when(near_low)(lambda: greet(lower))
    pl.when(near_high)(lambda: greet(higher))
    others = 5 + 3 * first.astype(jnp.int32) + (x == 1).astype(jnp.int32)
    for near in (z_high, z_low, near_low, near_high):
        others = others + near.astype(jnp.int32)

    pl.semaphore_wait(bar, others)

    def remote(source, target, send, recv, device):
        return pltpu.make_async_remote_copy(
            src_ref=source, dst_ref=target, send_sem=send, recv_sem=recv,
            device_id=device, device_id_type=MESH,
        )

    def straight(k):
        return remote(row(rotor, k), row(rin, k), r_send.at[k], r_recv.at[k], following)

    def through(k):
        i = THROUGH.index(k)
        return remote(row(rotor, k), row(relay_p, i), r_send.at[k], p_recv.at[i], up_x)

    def through_on(k):
        i = THROUGH.index(k)
        return remote(row(relay_p, i), row(rin, k), q_send.at[i], r_recv.at[k], up_y)

    def around(k):
        i = AROUND.index(k)
        return remote(row(rotor, k), row(relay_a, i), a_send.at[i], a_recv.at[i], down_x)

    def around_on(k, device):
        i = AROUND.index(k)
        return remote(row(relay_a, i), row(relay_b, i), b_send.at[i], b_recv.at[i], device)

    def around_end(k, device):
        i = AROUND.index(k)
        return remote(row(relay_b, i), row(rin, k), c_send.at[i], r_recv.at[k], device)

    low_edge = remote(row(vort, 0), vup, h_send.at[0], h_recv.at[0], preceding)
    high_edge = remote(row(comb, rows_az), row(comb, 0), h_send.at[1], h_recv.at[1], following)
    edges = remote(edge_s, edge_r, h_send.at[2], h_recv.at[2], following)

    def radial(side, device):
        return remote(
            edge_out.at[side], edge_in.at[side], e_send.at[side], e_recv.at[side], device
        )

    capacity = tbuf.shape[0] // n_ra
    group = 2 * capacity

    def tile_copy(d):
        to = (chip + d) % n_chip
        return remote(
            sbuf.at[pl.ds(pl.multiple_of(to * group, group), group)], trecv.at[chip],
            t_send.at[d], t_recv.at[d], (j, to * 2 + core),
        )

    exchange = remote(trecv, tsib, t_send.at[0], t_recv.at[0], sibling)

    def start_row(k):
        if k in THROUGH or k == AROUND_LAST:
            other_way = around if k == AROUND_LAST else through
            pl.when(last)(lambda: other_way(k).start())
            pl.when(jnp.logical_not(last))(lambda: straight(k).start())
        else:
            straight(k).start()

    start_row(0)
    start_row(7)
    around(3).start()
    start_row(5)
    around(4).start()

    loads[0].wait()
    for c in range(3):
        for k in range(rows_az):
            whole = rbuf[c, k].astype(jnp.float32)
            edge_f[c, k : k + 1] = whole[:1]
            edge_f[c, rows_az + k : rows_az + k + 1] = whole[rows_rad - 1 :]
    edge_s[...] = edge_f[...].astype(jnp.bfloat16)
    edges.start()
    start_row(1)
    low_edge.start()
    start_row(2)
    start_row(6)

    pl.when(z_low)(lambda: pl.semaphore_wait(up_sem, 1))
    pl.when(z_high)(
        lambda: pl.semaphore_signal(up_sem, inc=1, device_id=above, device_id_type=MESH)
    )
    @pl.when(jnp.logical_not(z_high))
    def _():
        for d in range(1, n_z):
            pl.semaphore_signal(down_sem, inc=1, device_id=(j, r - 2 * d), device_id_type=MESH)

    top = jnp.logical_and(core == 1, z == n_z - 1)
    tell = jnp.logical_and(top, chip >= n_z)
    pl.when(tell)(
        lambda: pl.semaphore_signal(
            seam_sem, inc=1, device_id=(j, r - n_ra // 2), device_id_type=MESH
        )
    )

    loads[2].wait()
    loads[3].wait()
    loads[4].wait()
    slots = tbuf.shape[0]
    slot = lax.broadcasted_iota(jnp.int32, (slots, slots), 0)
    lane = lax.broadcasted_iota(jnp.int32, (slots, slots), 1)
    ids = jnp.broadcast_to(idbuf[...].astype(jnp.float32), (slots, slots))
    id_col = jnp.sum(jnp.where(slot == lane, ids, 0.0), axis=1, keepdims=True)
    slot_n = lax.broadcasted_iota(jnp.int32, (slots, n_ra), 0)
    lane_n = lax.broadcasted_iota(jnp.int32, (slots, n_ra), 1)
    counts = jnp.broadcast_to(cntbuf[...].astype(jnp.float32), (slots, n_ra))
    count_col = jnp.sum(
        jnp.where(slot_n // capacity == lane_n, counts, 0.0), axis=1, keepdims=True
    )
    used = (slot % capacity).astype(jnp.float32) < count_col
    width = tbuf.shape[1]
    sbuf[:, :width] = tbuf[...]
    sbuf[:, width:] = jnp.where(used, id_col, -1.0)
    trecv[pl.ds(chip, 1)] = sbuf[pl.ds(pl.multiple_of(chip * group, group), group)][None]

    def send_tiles(low_z, high_z):
        @pl.when(jnp.logical_and(z >= low_z, z <= high_z))
        def _():
            pl.when(z_high)(lambda: pl.semaphore_wait(down_sem, 1))
            for d in range(1, n_chip):
                tile_copy(d).start()

    def take(k):
        straight(k).wait_recv()
        for c in range(3):
            comb[c, k + 1] = vbuf[c, k] + rin[c, k].astype(jnp.float32)

    def relay_through(k):
        @pl.when(first)
        def _():
            through(k).wait_recv()
            through_on(k).start()

    def relay_first(k):
        around(k).wait_recv()
        if k == AROUND_LAST:
            around_on(k, down_x).start()
        else:
            pl.when(x == 2)(lambda: around_on(k, at(1, y + 1)).start())
            pl.when(x != 2)(lambda: around_on(k, down_x).start())

    def relay_second(k):
        around_on(k, down_x).wait_recv()
        around_end(k, at(0, y + 1) if k == AROUND_LAST else down_x).start()

    send_tiles(n_z - 2, n_z - 1)
    loads[1].wait()
    for c in range(3):
        for k in range(rows_az):
            edge_out[1, c, k : k + 1] = vbuf[c, k, :1]
            edge_out[0, c, k : k + 1] = vbuf[c, k, rows_rad - 1 :]

    @pl.when(jnp.logical_not(has_low))
    def _():
        edge_in[0] = jnp.zeros_like(edge_in[0])

    @pl.when(jnp.logical_not(has_high))
    def _():
        edge_in[1] = jnp.zeros_like(edge_in[1])

    relay_through(0)
    relay_first(3)
    take(7)
    high_edge.start()
    send_tiles(n_z - 4, n_z - 3)
    relay_through(1)
    pl.when(x == 2)(lambda: relay_first(5))
    relay_first(4)
    relay_through(2)
    edges.wait_recv()
    for c in range(3):
        arrived = edge_r[c].astype(jnp.float32)
        edge_out[1, c] += arrived[:rows_az]
        edge_out[0, c] += arrived[rows_az:]
    in_run_low = jnp.logical_and(has_low, jnp.logical_not(seam_low))
    pl.when(seam_high)(lambda: pl.semaphore_wait(seam_sem, 1))
    pl.when(has_high)(lambda: radial(0, higher).start())
    pl.when(in_run_low)(lambda: radial(1, lower).start())
    send_tiles(0, n_z - 5)
    relay_through(6)
    relay_second(3)
    pl.when(x == 1)(lambda: relay_second(5))
    relay_second(4)
    take(0)
    take(1)
    take(5)

    @pl.when(seam_low)
    def _():
        tile_copy(1).wait_recv()
        radial(1, lower).start()

    pl.when(jnp.logical_not(seam_low))(lambda: tile_copy(1).wait_recv())
    for d in range(2, n_chip):
        tile_copy(d).wait_recv()
    exchange.start()

    axial = lax.broadcasted_iota(jnp.int32, (rows_rad, cells_ax), 1)
    radial_row = lax.broadcasted_iota(jnp.int32, (rows_rad, cells_ax), 0)
    position = (r * rows_rad + radial_row).astype(jnp.float32)
    inverse = 1.0 / (0.5 + (position + 0.5) / (rows_rad * n_ra))
    inverse_sq = inverse * inverse

    def stencil(k):
        v0 = cbuf[0, k].astype(jnp.float32)
        v1 = cbuf[1, k].astype(jnp.float32)
        v2 = cbuf[2, k].astype(jnp.float32)
        rad = (0.25 * DIFFUSION) * inverse - 0.5 * v0
        azi_even = DIFFUSION * inverse_sq
        azi_odd = 0.5 * v1 * inverse
        axi = 0.5 * v2
        middle = (1.0 - 4.0 * DIFFUSION) - (2.0 * DIFFUSION) * inverse_sq
        turn = (0.5 * DIFFUSION) * inverse_sq
        for c in range(3):
            f = comb[c, k + 1]
            nxt, prv = comb[c, k + 2], comb[c, k]
            up = pltpu.roll(f, rows_rad - 1, 0)
            up = jnp.where(radial_row == rows_rad - 1, edge_in[1, c, k : k + 1], up)
            down = pltpu.roll(f, 1, 0)
            down = jnp.where(radial_row == 0, edge_in[0, c, k : k + 1], down)
            right = jnp.where(axial == cells_ax - 1, 0.0, pltpu.roll(f, cells_ax - 1, 1))
            left = jnp.where(axial == 0, 0.0, pltpu.roll(f, 1, 1))
            total = middle * f + src[c, k]
            total = total + DIFFUSION * ((up + down) + (right + left))
            total = total + rad * (up - down) - axi * (right - left)
            total = total + azi_even * (nxt + prv) - azi_odd * (nxt - prv)
            if c == 0:
                total = total - (0.5 * turn) * f - turn * (comb[1, k + 2] - comb[1, k])
            elif c == 1:
                total = total - (0.5 * turn) * f + turn * (comb[0, k + 2] - comb[0, k])
            out[c, k] = total

    exchange.wait_recv()
    keep = (slot % group) // capacity == core
    halves = []
    for i, got in enumerate((trecv, tsib)):
        part = got[...].reshape(slots, width + slots)
        value = part[:, :width]
        top = value.astype(jnp.bfloat16)
        tmat[i * slots : (i + 1) * slots] = top
        tmat[(2 + i) * slots : (3 + i) * slots] = (value - top.astype(jnp.float32)).astype(
            jnp.bfloat16
        )
        halves.append(jnp.where(keep, part[:, width:], -1.0).T)
    blocks = jnp.concatenate(halves, axis=1)
    m = lax.broadcasted_iota(jnp.int32, blocks.shape, 0)
    per_row = cells_ax // TS
    local_block = (m % rows_rad) * per_row + m // rows_rad
    for a in range(rows_az):
        wanted = (local_block + a * rows_rad * per_row).astype(jnp.float32)
        hot = jnp.where(blocks == wanted, 1.0, 0.0).astype(jnp.bfloat16)
        placed = jnp.dot(
            jnp.concatenate([hot, hot], axis=1), tmat[...], preferred_element_type=jnp.float32
        )
        for b in range(per_row):
            for c in range(3):
                src[c, a, :, b * TS : (b + 1) * TS] = placed[
                    b * rows_rad : (b + 1) * rows_rad, c * TS : (c + 1) * TS
                ]

    loads[5].wait()
    low_edge.wait_recv()
    for c in range(3):
        comb[c, rows_az + 1] = vup[c, 0] + rbuf[c, 0].astype(jnp.float32)
    high_edge.wait_recv()
    pl.when(has_low)(lambda: radial(0, (j, r)).wait_recv())
    pl.when(has_high)(lambda: radial(1, (j, r)).wait_recv())
    stencil(0)
    take(3)
    take(4)
    stencil(4)
    take(2)
    stencil(1)
    stencil(2)
    stencil(3)
    take(6)
    stencil(7)
    stencil(5)
    stencil(6)

    for k in STRAIGHT:
        if k != AROUND_LAST:
            straight(k).wait_send()
    for k in AROUND:
        if k != AROUND_LAST:
            around(k).wait_send()
            around_on(k, down_x).wait_send()
            around_end(k, down_x).wait_send()
    pl.when(last)(lambda: around(AROUND_LAST).wait_send())
    pl.when(jnp.logical_not(last))(lambda: straight(AROUND_LAST).wait_send())
    pl.when(x == 2)(lambda: around_on(AROUND_LAST, down_x).wait_send())
    pl.when(x == 1)(lambda: around_end(AROUND_LAST, down_x).wait_send())

    @pl.when(first)
    def _():
        for k in THROUGH:
            through_on(k).wait_send()

    low_edge.wait_send()
    high_edge.wait_send()
    edges.wait_send()
    pl.when(has_high)(lambda: radial(0, (j, r)).wait_send())
    pl.when(has_low)(lambda: radial(1, (j, r)).wait_send())
    for d in range(1, n_chip):
        tile_copy(d).wait_send()
    exchange.wait_send()


def body(vorticity, rotor_field, courant, load_tiles, tile_block, tile_count):
    shape = vorticity.shape
    _, rows_az, rows_rad, cells_ax = shape
    slots, width = load_tiles.shape[2:]
    n_ra = lax.axis_size("ra")
    n_chip = n_ra // 2
    group = slots // n_chip
    one_row = (3, 1, rows_rad, cells_ax)

    def relay(n):
        return pltpu.VMEM((3, n, rows_rad, cells_ax), jnp.bfloat16)

    dma = pltpu.SemaphoreType.DMA
    around, through = len(AROUND), len(THROUGH)
    scratch = [
        pltpu.VMEM(shape, jnp.float32),
        pltpu.VMEM(shape, jnp.bfloat16),
        pltpu.VMEM(shape, jnp.bfloat16),
        pltpu.VMEM(shape, jnp.bfloat16),
        pltpu.VMEM((3, rows_az + 2, rows_rad, cells_ax), jnp.float32),
        pltpu.VMEM(shape, jnp.float32),
        pltpu.VMEM(one_row, jnp.float32),
        relay(around),
        relay(around),
        relay(through),
        pltpu.VMEM((3, 2 * rows_az, cells_ax), jnp.float32),
        pltpu.VMEM((3, 2 * rows_az, cells_ax), jnp.bfloat16),
        pltpu.VMEM((3, 2 * rows_az, cells_ax), jnp.bfloat16),
        pltpu.VMEM((2, 3, rows_az, cells_ax), jnp.float32),
        pltpu.VMEM((2, 3, rows_az, cells_ax), jnp.float32),
        pltpu.VMEM((slots, width), jnp.float32),
        pltpu.VMEM((1, slots), jnp.int32),
        pltpu.VMEM((1, n_ra), jnp.int32),
        pltpu.VMEM((slots, width + slots), jnp.float32),
        pltpu.VMEM((n_chip, group, width + slots), jnp.float32),
        pltpu.VMEM((n_chip, group, width + slots), jnp.float32),
        pltpu.VMEM((4 * slots, width), jnp.bfloat16),
        dma((6,)),
        dma((rows_az,)),
        dma((rows_az,)),
        dma((around,)),
        dma((around,)),
        dma((around,)),
        dma((around,)),
        dma((around,)),
        dma((through,)),
        dma((through,)),
        dma((3,)),
        dma((3,)),
        dma((2,)),
        dma((2,)),
        dma((n_chip,)),
        dma((n_chip,)),
        pltpu.SemaphoreType.REGULAR,
        pltpu.SemaphoreType.REGULAR,
        pltpu.SemaphoreType.REGULAR,
    ]
    return pl.pallas_call(
        kernel,
        name="step",
        out_shape=pltpu.VMEM(shape, jnp.float32),
        in_specs=[pl.BlockSpec(memory_space=pltpu.HBM)] * 6,
        out_specs=pl.BlockSpec(memory_space=pltpu.VMEM),
        scratch_shapes=scratch,
        compiler_params=pltpu.CompilerParams(
            collective_id=0, has_side_effects=True, vmem_limit_bytes=62 * 1024 * 1024
        ),
    )(vorticity, rotor_field, courant, load_tiles, tile_block, tile_count)


def solution(mesh):
    in_specs = (
        P(None, "azi", "ra", None),
        P(None, "azi", "ra", None),
        P(None, "azi", "ra", None),
        P("azi", "ra", None, None),
        P("azi", "ra", None),
        P("azi", "ra", None),
    )
    out_specs = P(None, "azi", "ra", None)
    return jax.shard_map(body, mesh=mesh, in_specs=in_specs, out_specs=out_specs, check_vma=False)
```

```python
import functools

import jax
import jax.numpy as jnp
from jax import lax
from jax.experimental import pallas as pl
from jax.experimental.pallas import tpu as pltpu
from jax.sharding import PartitionSpec as P

TS = 128
DIFFUSION = 0.15
MESH = pl.DeviceIdType.MESH
LEVELS = 32767.0
SMALLEST = 1e-30
CHIP_X = 4

AROUND = (3, 4, 5)
AROUND_LAST = 5
THROUGH = (0, 1, 2)
STRAIGHT = (0, 7, 5, 1, 2, 6)


def kernel(
    vort, rotor, cour, tiles, tile_id, tile_n, out,
    vbuf, cbuf, rbuf, rin, comb, src, code_out, code_in, scale_out, scale_in,
    relay_a, relay_b, relay_p, edge_f, edge_s, edge_r, edge_out, edge_in, seam_v, seam_r,
    tbuf, idbuf, cntbuf, sbuf, trecv, tsib, tmat,
    lsem, r_send, r_recv, a_send, a_recv, b_send, b_recv, c_send,
    p_recv, q_send, h_send, h_recv, e_send, e_recv, t_send, t_recv, up_sem, down_sem, seam_sem, seam_next,
):
    n_azi, n_ra = lax.axis_size("azi"), lax.axis_size("ra")
    n_y = n_azi // CHIP_X
    n_chip = n_ra // 2
    n_z = n_chip // 2
    rows_az, rows_rad, cells_ax = vbuf.shape[1:]
    j, r = lax.axis_index("azi"), lax.axis_index("ra")
    x, y = j % CHIP_X, j // CHIP_X
    chip, core = r // 2, r % 2
    z = chip % n_z
    first, last = x == 0, x == CHIP_X - 1
    has_low, has_high = r > 0, r < n_ra - 1
    z_low, z_high = z > 0, z < n_z - 1
    near_low = jnp.logical_and(core == 0, z_low)
    near_high = jnp.logical_and(core == 1, z_high)
    seam_low = jnp.logical_and(jnp.logical_and(core == 0, z == 0), has_low)
    seam_high = jnp.logical_and(jnp.logical_and(core == 1, z == n_z - 1), has_high)

    def at(xx, yy):
        return ((yy % n_y) * CHIP_X + xx % CHIP_X, r)

    following = ((j + 1) % n_azi, r)
    preceding = ((j + n_azi - 1) % n_azi, r)
    up_x, down_x = at(x + 1, y), at(x + 3, y)
    up_y, down_y = at(x, y + 1), at(x, y + n_y - 1)
    sibling = (j, chip * 2 + 1 - core)
    above, below = (j, r + 2), (j, r - 2)
    lower, higher = (j, r - 1), (j, r + 1)

    def local(ref, dst, k):
        return pltpu.make_async_copy(ref, dst, lsem.at[k])

    def row(ref, k):
        return ref.at[:, pl.ds(k, 1)]

    loads = [
        local(rotor, rbuf, 0),
        local(vort, vbuf, 1),
        local(tiles.at[0, 0], tbuf, 2),
        local(tile_id.at[0], idbuf, 3),
        local(tile_n.at[0], cntbuf, 4),
        local(cour, cbuf, 5),
    ]
    for load in loads:
        load.start()

    bar = pltpu.get_barrier_semaphore()

    def greet(device):
        pl.semaphore_signal(bar, inc=1, device_id=device, device_id_type=MESH)

    greet(following)
    greet(preceding)
    greet(sibling)
    greet((j, (r + n_ra // 2) % n_ra))
    pl.when(last)(lambda: greet(up_x))
    pl.when(first)(lambda: greet(down_x))
    pl.when(x == 2)(lambda: greet(at(1, y + 1)))
    pl.when(x == 1)(lambda: greet(at(2, y + n_y - 1)))
    pl.when(x == 1)(lambda: greet(at(0, y + 1)))

    @pl.when(first)
    def _():
        greet(up_y)
        greet(down_y)
        greet(at(1, y + n_y - 1))

    pl.when(z_high)(lambda: greet(above))
    pl.when(z_low)(lambda: greet(below))
    pl.when(near_low)(lambda: greet(lower))
    pl.when(near_high)(lambda: greet(higher))
    others = 5 + 3 * first.astype(jnp.int32) + (x == 1).astype(jnp.int32)
    for near in (z_high, z_low, near_low, near_high):
        others = others + near.astype(jnp.int32)

    pl.semaphore_wait(bar, others)

    def remote(source, target, send, recv, device):
        return pltpu.make_async_remote_copy(
            src_ref=source, dst_ref=target, send_sem=send, recv_sem=recv,
            device_id=device, device_id_type=MESH,
        )

    def straight(k):
        return remote(row(rotor, k), row(rin, k), r_send.at[k], r_recv.at[k], following)

    def through(k):
        i = THROUGH.index(k)
        return remote(row(rotor, k), row(relay_p, i), r_send.at[k], p_recv.at[i], up_x)

    def through_on(k):
        i = THROUGH.index(k)
        return remote(row(relay_p, i), row(rin, k), q_send.at[i], r_recv.at[k], up_y)

    def around(k):
        i = AROUND.index(k)
        return remote(row(rotor, k), row(relay_a, i), a_send.at[i], a_recv.at[i], down_x)

    def around_on(k, device):
        i = AROUND.index(k)
        return remote(row(relay_a, i), row(relay_b, i), b_send.at[i], b_recv.at[i], device)

    def around_end(k, device):
        i = AROUND.index(k)
        return remote(row(relay_b, i), row(rin, k), c_send.at[i], r_recv.at[k], device)

    def halo(side):
        to = (preceding, following)[side]
        return (
            remote(code_out.at[side], code_in.at[side], h_send.at[side], h_recv.at[side], to),
            remote(
                scale_out.at[side], scale_in.at[side], h_send.at[3 + side], h_recv.at[3 + side], to
            ),
        )

    def encode(side, values):
        scale_lane = lax.broadcasted_iota(jnp.int32, (rows_rad, TS), 1)
        scales = jnp.zeros((rows_rad, TS), jnp.float32)
        for c in range(3):
            value = values(c)
            largest = jnp.max(jnp.abs(value), axis=1, keepdims=True)
            largest = jnp.maximum(largest, SMALLEST)
            code = jnp.round(value * (LEVELS / largest))
            code_out[side, c] = code.astype(jnp.int32).astype(jnp.int16)
            scales = jnp.where(scale_lane == c, largest * (1.0 / LEVELS), scales)
        scale_out[side] = scales
        for copy in halo(side):
            copy.start()

    def decode(side, c):
        return code_in[side, c].astype(jnp.int32).astype(jnp.float32) * scale_in[side, :, c : c + 1]

    edges = remote(edge_s, edge_r, h_send.at[2], h_recv.at[2], following)

    def radial(side, device):
        return remote(
            edge_out.at[side], edge_in.at[side], e_send.at[side], e_recv.at[side], device
        )

    seam_own = remote(edge_out.at[0], seam_v, e_send.at[2], e_recv.at[2], higher)
    seam_turned = remote(edge_s, seam_r, e_send.at[3], e_recv.at[3], ((j + 1) % n_azi, r + 1))

    capacity = tbuf.shape[0] // n_ra
    group = 2 * capacity

    def tile_copy(d):
        to = (chip + d) % n_chip
        return remote(
            sbuf.at[pl.ds(pl.multiple_of(to * group, group), group)], trecv.at[chip],
            t_send.at[d], t_recv.at[d], (j, to * 2 + core),
        )

    exchange = remote(trecv, tsib, t_send.at[0], t_recv.at[0], sibling)

    def start_row(k):
        if k in THROUGH or k == AROUND_LAST:
            other_way = around if k == AROUND_LAST else through
            pl.when(last)(lambda: other_way(k).start())
            pl.when(jnp.logical_not(last))(lambda: straight(k).start())
        else:
            straight(k).start()

    start_row(0)
    start_row(7)
    around(3).start()
    start_row(5)
    around(4).start()

    pl.when(z_low)(lambda: pl.semaphore_wait(up_sem, 1))
    pl.when(z_high)(
        lambda: pl.semaphore_signal(up_sem, inc=1, device_id=above, device_id_type=MESH)
    )
    @pl.when(jnp.logical_not(z_high))
    def _():
        for d in range(1, n_z):
            pl.semaphore_signal(down_sem, inc=1, device_id=(j, r - 2 * d), device_id_type=MESH)

    top = jnp.logical_and(core == 1, z == n_z - 1)
    tell = jnp.logical_and(top, chip >= n_z)
    pl.when(tell)(
        lambda: pl.semaphore_signal(
            seam_sem, inc=1, device_id=(j, r - n_ra // 2), device_id_type=MESH
        )
    )

    loads[2].wait()
    loads[3].wait()
    loads[4].wait()
    slots = tbuf.shape[0]
    slot = lax.broadcasted_iota(jnp.int32, (slots, slots), 0)
    lane = lax.broadcasted_iota(jnp.int32, (slots, slots), 1)
    ids = jnp.broadcast_to(idbuf[...].astype(jnp.float32), (slots, slots))
    id_col = jnp.sum(jnp.where(slot == lane, ids, 0.0), axis=1, keepdims=True)
    slot_n = lax.broadcasted_iota(jnp.int32, (slots, n_ra), 0)
    lane_n = lax.broadcasted_iota(jnp.int32, (slots, n_ra), 1)
    counts = jnp.broadcast_to(cntbuf[...].astype(jnp.float32), (slots, n_ra))
    count_col = jnp.sum(
        jnp.where(slot_n // capacity == lane_n, counts, 0.0), axis=1, keepdims=True
    )
    used = (slot % capacity).astype(jnp.float32) < count_col
    width = tbuf.shape[1]
    sbuf[:, :width] = tbuf[...]
    sbuf[:, width:] = jnp.where(used, id_col, -1.0)
    trecv[pl.ds(chip, 1)] = sbuf[pl.ds(pl.multiple_of(chip * group, group), group)][None]

    def send_tiles(low_z, high_z):
        @pl.when(jnp.logical_and(z >= low_z, z <= high_z))
        def _():
            pl.when(z_high)(lambda: pl.semaphore_wait(down_sem, 1))
            for d in range(1, n_chip):
                tile_copy(d).start()

    send_tiles(n_z - 2, n_z - 1)

    loads[0].wait()
    for c in range(3):
        for k in range(rows_az):
            whole = rbuf[c, k].astype(jnp.float32)
            edge_f[c, k : k + 1] = whole[:1]
            edge_f[c, rows_az + k : rows_az + k + 1] = whole[rows_rad - 1 :]
    edge_s[...] = edge_f[...].astype(jnp.bfloat16)
    @pl.when(seam_high)
    def _():
        pl.semaphore_wait(seam_sem, 1)
        pl.semaphore_signal(seam_next, inc=1, device_id=preceding, device_id_type=MESH)
        pl.semaphore_wait(seam_next, 1)
        seam_turned.start()

    edges.start()
    loads[1].wait()
    for c in range(3):
        for k in range(rows_az):
            edge_out[1, c, k : k + 1] = vbuf[c, k, :1]
            edge_out[0, c, k : k + 1] = vbuf[c, k, rows_rad - 1 :]

    pl.when(seam_high)(lambda: seam_own.start())
    start_row(1)
    encode(0, lambda c: vbuf[c, 0])
    start_row(2)
    start_row(6)

    def take(k):
        straight(k).wait_recv()
        for c in range(3):
            comb[c, k + 1] = vbuf[c, k] + rin[c, k].astype(jnp.float32)

    def relay_through(k):
        @pl.when(first)
        def _():
            through(k).wait_recv()
            through_on(k).start()

    def relay_first(k):
        around(k).wait_recv()
        if k == AROUND_LAST:
            around_on(k, down_x).start()
        else:
            pl.when(x == 2)(lambda: around_on(k, at(1, y + 1)).start())
            pl.when(x != 2)(lambda: around_on(k, down_x).start())

    def relay_second(k):
        around_on(k, down_x).wait_recv()
        around_end(k, at(0, y + 1) if k == AROUND_LAST else down_x).start()

    @pl.when(jnp.logical_not(has_low))
    def _():
        edge_in[0] = jnp.zeros_like(edge_in[0])

    @pl.when(jnp.logical_not(has_high))
    def _():
        edge_in[1] = jnp.zeros_like(edge_in[1])

    send_tiles(n_z - 4, n_z - 3)
    relay_through(0)
    relay_first(3)
    take(7)
    encode(1, lambda c: comb[c, rows_az])
    send_tiles(2, n_z - 5)
    relay_through(1)
    pl.when(x == 2)(lambda: relay_first(5))
    relay_first(4)
    relay_through(2)
    send_tiles(0, 1)
    edges.wait_recv()
    pl.when(seam_high)(lambda: seam_own.wait_send())
    for c in range(3):
        arrived = edge_r[c].astype(jnp.float32)
        edge_out[1, c] += arrived[:rows_az]
        edge_out[0, c] += arrived[rows_az:]
    in_run_low = jnp.logical_and(has_low, jnp.logical_not(seam_low))
    in_run_high = jnp.logical_and(has_high, jnp.logical_not(seam_high))
    pl.when(in_run_high)(lambda: radial(0, higher).start())
    pl.when(in_run_low)(lambda: radial(1, lower).start())
    relay_second(3)
    pl.when(x == 1)(lambda: relay_second(5))
    relay_second(4)
    take(0)
    take(1)
    take(5)

    @pl.when(seam_low)
    def _():
        tile_copy(1).wait_recv()
        radial(1, lower).start()

    pl.when(jnp.logical_not(seam_low))(lambda: tile_copy(1).wait_recv())
    for d in range(2, n_chip):
        tile_copy(d).wait_recv()
    exchange.start()

    axial = lax.broadcasted_iota(jnp.int32, (rows_rad, cells_ax), 1)
    radial_row = lax.broadcasted_iota(jnp.int32, (rows_rad, cells_ax), 0)
    position = (r * rows_rad + radial_row).astype(jnp.float32)
    inverse = 1.0 / (0.5 + (position + 0.5) / (rows_rad * n_ra))
    inverse_sq = inverse * inverse

    def stencil(k):
        v0 = cbuf[0, k].astype(jnp.float32)
        v1 = cbuf[1, k].astype(jnp.float32)
        v2 = cbuf[2, k].astype(jnp.float32)
        rad = (0.25 * DIFFUSION) * inverse - 0.5 * v0
        azi_even = DIFFUSION * inverse_sq
        azi_odd = 0.5 * v1 * inverse
        axi = 0.5 * v2
        middle = (1.0 - 4.0 * DIFFUSION) - (2.0 * DIFFUSION) * inverse_sq
        turn = (0.5 * DIFFUSION) * inverse_sq
        for c in range(3):
            f = comb[c, k + 1]
            nxt, prv = comb[c, k + 2], comb[c, k]
            up = pltpu.roll(f, rows_rad - 1, 0)
            up = jnp.where(radial_row == rows_rad - 1, edge_in[1, c, k : k + 1], up)
            down = pltpu.roll(f, 1, 0)
            down = jnp.where(radial_row == 0, edge_in[0, c, k : k + 1], down)
            right = jnp.where(axial == cells_ax - 1, 0.0, pltpu.roll(f, cells_ax - 1, 1))
            left = jnp.where(axial == 0, 0.0, pltpu.roll(f, 1, 1))
            total = middle * f + src[c, k]
            total = total + DIFFUSION * ((up + down) + (right + left))
            total = total + rad * (up - down) - axi * (right - left)
            total = total + azi_even * (nxt + prv) - azi_odd * (nxt - prv)
            if c == 0:
                total = total - (0.5 * turn) * f - turn * (comb[1, k + 2] - comb[1, k])
            elif c == 1:
                total = total - (0.5 * turn) * f + turn * (comb[0, k + 2] - comb[0, k])
            out[c, k] = total

    exchange.wait_recv()
    keep = (slot % group) // capacity == core
    halves = []
    for i, got in enumerate((trecv, tsib)):
        part = got[...].reshape(slots, width + slots)
        value = part[:, :width]
        top = value.astype(jnp.bfloat16)
        tmat[i * slots : (i + 1) * slots] = top
        tmat[(2 + i) * slots : (3 + i) * slots] = (value - top.astype(jnp.float32)).astype(
            jnp.bfloat16
        )
        halves.append(jnp.where(keep, part[:, width:], -1.0).T)
    blocks = jnp.concatenate(halves, axis=1)
    m = lax.broadcasted_iota(jnp.int32, blocks.shape, 0)
    per_row = cells_ax // TS
    local_block = (m % rows_rad) * per_row + m // rows_rad
    for a in range(rows_az):
        wanted = (local_block + a * rows_rad * per_row).astype(jnp.float32)
        hot = jnp.where(blocks == wanted, 1.0, 0.0).astype(jnp.bfloat16)
        placed = jnp.dot(
            jnp.concatenate([hot, hot], axis=1), tmat[...], preferred_element_type=jnp.float32
        )
        for b in range(per_row):
            for c in range(3):
                src[c, a, :, b * TS : (b + 1) * TS] = placed[
                    b * rows_rad : (b + 1) * rows_rad, c * TS : (c + 1) * TS
                ]

    loads[5].wait()
    for copy in (*halo(0), *halo(1)):
        copy.wait_recv()
    for c in range(3):
        comb[c, rows_az + 1] = decode(0, c) + rbuf[c, 0].astype(jnp.float32)
        comb[c, 0] = decode(1, c)
    pl.when(in_run_low)(lambda: radial(0, (j, r)).wait_recv())

    @pl.when(seam_low)
    def _():
        seam_own.wait_recv()
        seam_turned.wait_recv()
        for c in range(3):
            edge_in[0, c] = seam_v[c] + seam_r[c].astype(jnp.float32)[rows_az:]

    pl.when(has_high)(lambda: radial(1, (j, r)).wait_recv())
    stencil(0)
    take(3)
    take(4)
    stencil(4)
    take(2)
    stencil(1)
    stencil(2)
    stencil(3)
    take(6)
    stencil(7)
    stencil(5)
    stencil(6)

    for k in STRAIGHT:
        if k != AROUND_LAST:
            straight(k).wait_send()
    for k in AROUND:
        if k != AROUND_LAST:
            around(k).wait_send()
            around_on(k, down_x).wait_send()
            around_end(k, down_x).wait_send()
    pl.when(last)(lambda: around(AROUND_LAST).wait_send())
    pl.when(jnp.logical_not(last))(lambda: straight(AROUND_LAST).wait_send())
    pl.when(x == 2)(lambda: around_on(AROUND_LAST, down_x).wait_send())
    pl.when(x == 1)(lambda: around_end(AROUND_LAST, down_x).wait_send())

    @pl.when(first)
    def _():
        for k in THROUGH:
            through_on(k).wait_send()

    for copy in (*halo(0), *halo(1)):
        copy.wait_send()
    edges.wait_send()
    pl.when(in_run_high)(lambda: radial(0, (j, r)).wait_send())
    pl.when(seam_high)(lambda: seam_turned.wait_send())
    pl.when(has_low)(lambda: radial(1, (j, r)).wait_send())
    for d in range(1, n_chip):
        tile_copy(d).wait_send()
    exchange.wait_send()


def body(vorticity, rotor_field, courant, load_tiles, tile_block, tile_count):
    shape = vorticity.shape
    _, rows_az, rows_rad, cells_ax = shape
    slots, width = load_tiles.shape[2:]
    n_ra = lax.axis_size("ra")
    n_chip = n_ra // 2
    group = slots // n_chip

    def relay(n):
        return pltpu.VMEM((3, n, rows_rad, cells_ax), jnp.bfloat16)

    dma = pltpu.SemaphoreType.DMA
    around, through = len(AROUND), len(THROUGH)
    scratch = [
        pltpu.VMEM(shape, jnp.float32),
        pltpu.VMEM(shape, jnp.bfloat16),
        pltpu.VMEM(shape, jnp.bfloat16),
        pltpu.VMEM(shape, jnp.bfloat16),
        pltpu.VMEM((3, rows_az + 2, rows_rad, cells_ax), jnp.float32),
        pltpu.VMEM(shape, jnp.float32),
        pltpu.VMEM((2, 3, rows_rad, cells_ax), jnp.int16),
        pltpu.VMEM((2, 3, rows_rad, cells_ax), jnp.int16),
        pltpu.VMEM((2, rows_rad, TS), jnp.float32),
        pltpu.VMEM((2, rows_rad, TS), jnp.float32),
        relay(around),
        relay(around),
        relay(through),
        pltpu.VMEM((3, 2 * rows_az, cells_ax), jnp.float32),
        pltpu.VMEM((3, 2 * rows_az, cells_ax), jnp.bfloat16),
        pltpu.VMEM((3, 2 * rows_az, cells_ax), jnp.bfloat16),
        pltpu.VMEM((2, 3, rows_az, cells_ax), jnp.float32),
        pltpu.VMEM((2, 3, rows_az, cells_ax), jnp.float32),
        pltpu.VMEM((3, rows_az, cells_ax), jnp.float32),
        pltpu.VMEM((3, 2 * rows_az, cells_ax), jnp.bfloat16),
        pltpu.VMEM((slots, width), jnp.float32),
        pltpu.VMEM((1, slots), jnp.int32),
        pltpu.VMEM((1, n_ra), jnp.int32),
        pltpu.VMEM((slots, width + slots), jnp.float32),
        pltpu.VMEM((n_chip, group, width + slots), jnp.float32),
        pltpu.VMEM((n_chip, group, width + slots), jnp.float32),
        pltpu.VMEM((4 * slots, width), jnp.bfloat16),
        dma((6,)),
        dma((rows_az,)),
        dma((rows_az,)),
        dma((around,)),
        dma((around,)),
        dma((around,)),
        dma((around,)),
        dma((around,)),
        dma((through,)),
        dma((through,)),
        dma((5,)),
        dma((5,)),
        dma((4,)),
        dma((4,)),
        dma((n_chip,)),
        dma((n_chip,)),
        pltpu.SemaphoreType.REGULAR,
        pltpu.SemaphoreType.REGULAR,
        pltpu.SemaphoreType.REGULAR,
        pltpu.SemaphoreType.REGULAR,
    ]
    return pl.pallas_call(
        kernel,
        name="step",
        out_shape=pltpu.VMEM(shape, jnp.float32),
        in_specs=[pl.BlockSpec(memory_space=pltpu.HBM)] * 6,
        out_specs=pl.BlockSpec(memory_space=pltpu.VMEM),
        scratch_shapes=scratch,
        compiler_params=pltpu.CompilerParams(
            collective_id=0, has_side_effects=True, vmem_limit_bytes=62 * 1024 * 1024
        ),
    )(vorticity, rotor_field, courant, load_tiles, tile_block, tile_count)


def solution(mesh):
    in_specs = (
        P(None, "azi", "ra", None),
        P(None, "azi", "ra", None),
        P(None, "azi", "ra", None),
        P("azi", "ra", None, None),
        P("azi", "ra", None),
        P("azi", "ra", None),
    )
    out_specs = P(None, "azi", "ra", None)
    return jax.shard_map(body, mesh=mesh, in_specs=in_specs, out_specs=out_specs, check_vma=False)
```

```python
import functools

import jax
import jax.numpy as jnp
from jax import lax
from jax.experimental import pallas as pl
from jax.experimental.pallas import tpu as pltpu
from jax.sharding import PartitionSpec as P

TS = 128
DIFFUSION = 0.15
MESH = pl.DeviceIdType.MESH
SOURCE_AFTER = (0, 1, 2, 3, 4)
LEVELS = 32767.0
SMALLEST = 1e-30
CHIP_X = 4

AROUND = (3, 4, 5)
AROUND_LAST = 5
THROUGH = (0, 1, 2)
STRAIGHT = (0, 7, 5, 1, 2, 6)


def kernel(
    vort, rotor, cour, tiles, tile_id, tile_n, out,
    vbuf, cbuf, rbuf, rin, comb, src, code_out, code_in, scale_out, scale_in,
    relay_a, relay_b, relay_p, edge_f, edge_s, edge_r, edge_out, edge_in, seam_v, seam_r,
    tbuf, idbuf, cntbuf, sbuf, trecv, tsib, tmat,
    lsem, r_send, r_recv, a_send, a_recv, b_send, b_recv, c_send,
    p_recv, q_send, h_send, h_recv, e_send, e_recv, t_send, t_recv, up_sem, down_sem, above_sem, seam_sem, seam_next,
):
    n_azi, n_ra = lax.axis_size("azi"), lax.axis_size("ra")
    n_y = n_azi // CHIP_X
    n_chip = n_ra // 2
    n_z = n_chip // 2
    rows_az, rows_rad, cells_ax = vbuf.shape[1:]
    j, r = lax.axis_index("azi"), lax.axis_index("ra")
    x, y = j % CHIP_X, j // CHIP_X
    chip, core = r // 2, r % 2
    z = chip % n_z
    first, last = x == 0, x == CHIP_X - 1
    has_low, has_high = r > 0, r < n_ra - 1
    z_low, z_high = z > 0, z < n_z - 1
    near_low = jnp.logical_and(core == 0, z_low)
    near_high = jnp.logical_and(core == 1, z_high)
    seam_low = jnp.logical_and(jnp.logical_and(core == 0, z == 0), has_low)
    seam_high = jnp.logical_and(jnp.logical_and(core == 1, z == n_z - 1), has_high)

    def at(xx, yy):
        return ((yy % n_y) * CHIP_X + xx % CHIP_X, r)

    following = ((j + 1) % n_azi, r)
    preceding = ((j + n_azi - 1) % n_azi, r)
    up_x, down_x = at(x + 1, y), at(x + 3, y)
    up_y, down_y = at(x, y + 1), at(x, y + n_y - 1)
    sibling = (j, chip * 2 + 1 - core)
    above, below = (j, r + 2), (j, r - 2)
    lower, higher = (j, r - 1), (j, r + 1)

    def local(ref, dst, k):
        return pltpu.make_async_copy(ref, dst, lsem.at[k])

    def row(ref, k):
        return ref.at[:, pl.ds(k, 1)]

    loads = [
        local(rotor, rbuf, 0),
        local(vort, vbuf, 1),
        local(tiles.at[0, 0], tbuf, 2),
        local(tile_id.at[0], idbuf, 3),
        local(tile_n.at[0], cntbuf, 4),
        local(cour, cbuf, 5),
    ]
    for load in loads:
        load.start()

    bar = pltpu.get_barrier_semaphore()

    def greet(device):
        pl.semaphore_signal(bar, inc=1, device_id=device, device_id_type=MESH)

    greet(following)
    greet(preceding)
    greet(sibling)
    greet((j, (r + n_ra // 2) % n_ra))
    pl.when(last)(lambda: greet(up_x))
    pl.when(first)(lambda: greet(down_x))
    pl.when(x == 2)(lambda: greet(at(1, y + 1)))
    pl.when(x == 1)(lambda: greet(at(2, y + n_y - 1)))
    pl.when(x == 1)(lambda: greet(at(0, y + 1)))

    @pl.when(first)
    def _():
        greet(up_y)
        greet(down_y)
        greet(at(1, y + n_y - 1))

    pl.when(z_high)(lambda: greet(above))
    pl.when(near_high)(lambda: greet(higher))
    others = 5 + 3 * first.astype(jnp.int32) + (x == 1).astype(jnp.int32)
    for near in (z_low, near_low):
        others = others + near.astype(jnp.int32)

    pl.semaphore_wait(bar, others)

    def remote(source, target, send, recv, device):
        return pltpu.make_async_remote_copy(
            src_ref=source, dst_ref=target, send_sem=send, recv_sem=recv,
            device_id=device, device_id_type=MESH,
        )

    def straight(k):
        return remote(row(rotor, k), row(rin, k), r_send.at[k], r_recv.at[k], following)

    def through(k):
        i = THROUGH.index(k)
        return remote(row(rotor, k), row(relay_p, i), r_send.at[k], p_recv.at[i], up_x)

    def through_on(k):
        i = THROUGH.index(k)
        return remote(row(relay_p, i), row(rin, k), q_send.at[i], r_recv.at[k], up_y)

    def around(k):
        i = AROUND.index(k)
        return remote(row(rotor, k), row(relay_a, i), a_send.at[i], a_recv.at[i], down_x)

    def around_on(k, device):
        i = AROUND.index(k)
        return remote(row(relay_a, i), row(relay_b, i), b_send.at[i], b_recv.at[i], device)

    def around_end(k, device):
        i = AROUND.index(k)
        return remote(row(relay_b, i), row(rin, k), c_send.at[i], r_recv.at[k], device)

    def halo(side):
        to = (preceding, following)[side]
        return (
            remote(code_out.at[side], code_in.at[side], h_send.at[side], h_recv.at[side], to),
            remote(
                scale_out.at[side], scale_in.at[side], h_send.at[3 + side], h_recv.at[3 + side], to
            ),
        )

    def encode(side, values):
        scale_lane = lax.broadcasted_iota(jnp.int32, (rows_rad, TS), 1)
        scales = jnp.zeros((rows_rad, TS), jnp.float32)
        for c in range(3):
            value = values(c)
            largest = jnp.max(jnp.abs(value), axis=1, keepdims=True)
            largest = jnp.maximum(largest, SMALLEST)
            code = jnp.round(value * (LEVELS / largest))
            code_out[side, c] = code.astype(jnp.int32).astype(jnp.int16)
            scales = jnp.where(scale_lane == c, largest * (1.0 / LEVELS), scales)
        scale_out[side] = scales
        for copy in halo(side):
            copy.start()

    def decode(side, c):
        return code_in[side, c].astype(jnp.int32).astype(jnp.float32) * scale_in[side, :, c : c + 1]

    edges = remote(edge_s, edge_r, h_send.at[2], h_recv.at[2], following)

    def radial(side, device):
        return remote(
            edge_out.at[side], edge_in.at[side], e_send.at[side], e_recv.at[side], device
        )

    seam_own = remote(edge_out.at[0], seam_v, e_send.at[2], e_recv.at[2], higher)
    seam_turned = remote(edge_s, seam_r, e_send.at[3], e_recv.at[3], ((j + 1) % n_azi, r + 1))

    capacity = tbuf.shape[0] // n_ra
    group = 2 * capacity

    def tile_copy(d):
        to = (chip + d) % n_chip
        return remote(
            sbuf.at[pl.ds(pl.multiple_of(to * group, group), group)], trecv.at[chip],
            t_send.at[d], t_recv.at[d], (j, to * 2 + core),
        )

    exchange = remote(trecv, tsib, t_send.at[0], t_recv.at[0], sibling)

    def start_row(k):
        if k in THROUGH or k == AROUND_LAST:
            other_way = around if k == AROUND_LAST else through
            pl.when(last)(lambda: other_way(k).start())
            pl.when(jnp.logical_not(last))(lambda: straight(k).start())
        else:
            straight(k).start()

    start_row(0)
    start_row(7)
    around(3).start()
    start_row(5)
    around(4).start()

    pl.when(z_low)(
        lambda: pl.semaphore_signal(above_sem, inc=1, device_id=below, device_id_type=MESH)
    )
    pl.when(z_low)(lambda: pl.semaphore_wait(up_sem, 1))

    @pl.when(z_high)
    def _():
        pl.semaphore_wait(above_sem, 1)
        pl.semaphore_signal(up_sem, inc=1, device_id=above, device_id_type=MESH)

    @pl.when(jnp.logical_not(z_high))
    def _():
        for d in range(1, n_z):
            pl.semaphore_signal(down_sem, inc=1, device_id=(j, r - 2 * d), device_id_type=MESH)

    top = jnp.logical_and(core == 1, z == n_z - 1)
    tell = jnp.logical_and(top, chip >= n_z)
    pl.when(tell)(
        lambda: pl.semaphore_signal(
            seam_sem, inc=1, device_id=(j, r - n_ra // 2), device_id_type=MESH
        )
    )

    loads[2].wait()
    loads[3].wait()
    loads[4].wait()
    slots = tbuf.shape[0]
    slot = lax.broadcasted_iota(jnp.int32, (slots, slots), 0)
    lane = lax.broadcasted_iota(jnp.int32, (slots, slots), 1)
    ids = jnp.broadcast_to(idbuf[...].astype(jnp.float32), (slots, slots))
    id_col = jnp.sum(jnp.where(slot == lane, ids, 0.0), axis=1, keepdims=True)
    slot_n = lax.broadcasted_iota(jnp.int32, (slots, n_ra), 0)
    lane_n = lax.broadcasted_iota(jnp.int32, (slots, n_ra), 1)
    counts = jnp.broadcast_to(cntbuf[...].astype(jnp.float32), (slots, n_ra))
    count_col = jnp.sum(
        jnp.where(slot_n // capacity == lane_n, counts, 0.0), axis=1, keepdims=True
    )
    used = (slot % capacity).astype(jnp.float32) < count_col
    width = tbuf.shape[1]
    sbuf[:, :width] = tbuf[...]
    sbuf[:, width:] = jnp.where(used, id_col, -1.0)
    trecv[pl.ds(chip, 1)] = sbuf[pl.ds(pl.multiple_of(chip * group, group), group)][None]

    def send_tiles(low_z, high_z):
        @pl.when(jnp.logical_and(z >= low_z, z <= high_z))
        def _():
            pl.when(z_high)(lambda: pl.semaphore_wait(down_sem, 1))
            for d in range(1, n_chip):
                tile_copy(d).start()

    send_tiles(n_z - 2, n_z - 1)

    loads[0].wait()
    for c in range(3):
        for k in range(rows_az):
            whole = rbuf[c, k].astype(jnp.float32)
            edge_f[c, k : k + 1] = whole[:1]
            edge_f[c, rows_az + k : rows_az + k + 1] = whole[rows_rad - 1 :]
    edge_s[...] = edge_f[...].astype(jnp.bfloat16)
    @pl.when(seam_high)
    def _():
        pl.semaphore_wait(seam_sem, 1)
        pl.semaphore_signal(seam_next, inc=1, device_id=preceding, device_id_type=MESH)
        pl.semaphore_wait(seam_next, 1)
        seam_turned.start()

    edges.start()
    loads[1].wait()
    for c in range(3):
        for k in range(rows_az):
            edge_out[1, c, k : k + 1] = vbuf[c, k, :1]
            edge_out[0, c, k : k + 1] = vbuf[c, k, rows_rad - 1 :]

    pl.when(seam_high)(lambda: seam_own.start())
    start_row(1)
    encode(0, lambda c: vbuf[c, 0])
    start_row(2)
    start_row(6)

    def take(k):
        straight(k).wait_recv()
        for c in range(3):
            comb[c, k + 1] = vbuf[c, k] + rin[c, k].astype(jnp.float32)

    def relay_through(k):
        @pl.when(first)
        def _():
            through(k).wait_recv()
            through_on(k).start()

    def relay_first(k):
        around(k).wait_recv()
        if k == AROUND_LAST:
            around_on(k, down_x).start()
        else:
            pl.when(x == 2)(lambda: around_on(k, at(1, y + 1)).start())
            pl.when(x != 2)(lambda: around_on(k, down_x).start())

    def relay_second(k):
        around_on(k, down_x).wait_recv()
        around_end(k, at(0, y + 1) if k == AROUND_LAST else down_x).start()

    in_run_low = jnp.logical_and(has_low, jnp.logical_not(seam_low))
    in_run_high = jnp.logical_and(has_high, jnp.logical_not(seam_high))

    @pl.when(jnp.logical_not(in_run_low))
    def _():
        edge_in[0] = jnp.zeros_like(edge_in[0])

    @pl.when(jnp.logical_not(has_high))
    def _():
        edge_in[1] = jnp.zeros_like(edge_in[1])

    send_tiles(n_z - 4, n_z - 3)
    relay_through(0)
    relay_first(3)
    take(7)
    encode(1, lambda c: comb[c, rows_az])
    send_tiles(2, n_z - 5)
    relay_through(1)
    pl.when(x == 2)(lambda: relay_first(5))
    relay_first(4)
    relay_through(2)
    send_tiles(0, 1)
    edges.wait_recv()
    pl.when(seam_high)(lambda: seam_own.wait_send())
    for c in range(3):
        arrived = edge_r[c].astype(jnp.float32)
        edge_out[1, c] += arrived[:rows_az]
        edge_out[0, c] += arrived[rows_az:]
    pl.when(in_run_high)(lambda: radial(0, higher).start())
    pl.when(in_run_low)(lambda: radial(1, lower).start())
    relay_second(3)
    pl.when(x == 1)(lambda: relay_second(5))
    relay_second(4)
    take(0)
    take(1)

    @pl.when(seam_low)
    def _():
        tile_copy(1).wait_recv()
        radial(1, lower).start()

    pl.when(jnp.logical_not(seam_low))(lambda: tile_copy(1).wait_recv())
    for d in range(2, n_chip):
        tile_copy(d).wait_recv()
    exchange.start()

    axial = lax.broadcasted_iota(jnp.int32, (rows_rad, cells_ax), 1)
    radial_row = lax.broadcasted_iota(jnp.int32, (rows_rad, cells_ax), 0)
    position = (r * rows_rad + radial_row).astype(jnp.float32)
    inverse = 1.0 / (0.5 + (position + 0.5) / (rows_rad * n_ra))
    inverse_sq = inverse * inverse

    def stencil(k, with_source):
        v0 = cbuf[0, k].astype(jnp.float32)
        v1 = cbuf[1, k].astype(jnp.float32)
        v2 = cbuf[2, k].astype(jnp.float32)
        rad = (0.25 * DIFFUSION) * inverse - 0.5 * v0
        azi_even = DIFFUSION * inverse_sq
        azi_odd = 0.5 * v1 * inverse
        axi = 0.5 * v2
        middle = (1.0 - 4.0 * DIFFUSION) - (2.0 * DIFFUSION) * inverse_sq
        turn = (0.5 * DIFFUSION) * inverse_sq
        for c in range(3):
            f = comb[c, k + 1]
            nxt, prv = comb[c, k + 2], comb[c, k]
            up = pltpu.roll(f, rows_rad - 1, 0)
            up = jnp.where(radial_row == rows_rad - 1, edge_in[1, c, k : k + 1], up)
            down = pltpu.roll(f, 1, 0)
            down = jnp.where(radial_row == 0, edge_in[0, c, k : k + 1], down)
            right = jnp.where(axial == cells_ax - 1, 0.0, pltpu.roll(f, cells_ax - 1, 1))
            left = jnp.where(axial == 0, 0.0, pltpu.roll(f, 1, 1))
            total = middle * f
            if with_source:
                total = total + src[c, k]
            total = total + DIFFUSION * ((up + down) + (right + left))
            total = total + rad * (up - down) - axi * (right - left)
            total = total + azi_even * (nxt + prv) - azi_odd * (nxt - prv)
            if c == 0:
                total = total - (0.5 * turn) * f - turn * (comb[1, k + 2] - comb[1, k])
            elif c == 1:
                total = total - (0.5 * turn) * f + turn * (comb[0, k + 2] - comb[0, k])
            out[c, k] = total

    loads[5].wait()
    take(3)
    pl.when(in_run_low)(lambda: radial(0, (j, r)).wait_recv())
    pl.when(has_high)(lambda: radial(1, (j, r)).wait_recv())
    take(2)
    stencil(1, False)
    stencil(2, False)
    for copy in (*halo(0), *halo(1)):
        copy.wait_recv()
    for c in range(3):
        comb[c, rows_az + 1] = decode(0, c) + rbuf[c, 0].astype(jnp.float32)
        comb[c, 0] = decode(1, c)
    stencil(0, False)
    take(5)
    take(4)
    stencil(3, False)
    stencil(4, False)

    exchange.wait_recv()
    keep = (slot % group) // capacity == core
    halves = []
    for i, got in enumerate((trecv, tsib)):
        part = got[...].reshape(slots, width + slots)
        value = part[:, :width]
        top = value.astype(jnp.bfloat16)
        tmat[i * slots : (i + 1) * slots] = top
        tmat[(2 + i) * slots : (3 + i) * slots] = (value - top.astype(jnp.float32)).astype(
            jnp.bfloat16
        )
        halves.append(jnp.where(keep, part[:, width:], -1.0).T)
    blocks = jnp.concatenate(halves, axis=1)
    m = lax.broadcasted_iota(jnp.int32, blocks.shape, 0)
    per_row = cells_ax // TS
    local_block = (m % rows_rad) * per_row + m // rows_rad
    for a in range(rows_az):
        wanted = (local_block + a * rows_rad * per_row).astype(jnp.float32)
        hot = jnp.where(blocks == wanted, 1.0, 0.0).astype(jnp.bfloat16)
        placed = jnp.dot(
            jnp.concatenate([hot, hot], axis=1), tmat[...], preferred_element_type=jnp.float32
        )
        for b in range(per_row):
            for c in range(3):
                block = placed[b * rows_rad : (b + 1) * rows_rad, c * TS : (c + 1) * TS]
                if a in SOURCE_AFTER:
                    out[c, a, :, b * TS : (b + 1) * TS] += block
                else:
                    src[c, a, :, b * TS : (b + 1) * TS] = block

    take(6)
    stencil(7, True)
    stencil(5, True)
    stencil(6, True)

    @pl.when(seam_low)
    def _():
        seam_own.wait_recv()
        seam_turned.wait_recv()
        edge_inverse = inverse[:1]
        for c in range(3):
            arrived = seam_v[c] + seam_r[c].astype(jnp.float32)[rows_az:]
            for k in range(rows_az):
                v0 = cbuf[0, k].astype(jnp.float32)[:1]
                weight = DIFFUSION - (0.25 * DIFFUSION) * edge_inverse + 0.5 * v0
                out[c, k, :1] += weight * arrived[k : k + 1]

    for k in STRAIGHT:
        if k != AROUND_LAST:
            straight(k).wait_send()
    for k in AROUND:
        if k != AROUND_LAST:
            around(k).wait_send()
            around_on(k, down_x).wait_send()
            around_end(k, down_x).wait_send()
    pl.when(last)(lambda: around(AROUND_LAST).wait_send())
    pl.when(jnp.logical_not(last))(lambda: straight(AROUND_LAST).wait_send())
    pl.when(x == 2)(lambda: around_on(AROUND_LAST, down_x).wait_send())
    pl.when(x == 1)(lambda: around_end(AROUND_LAST, down_x).wait_send())

    @pl.when(first)
    def _():
        for k in THROUGH:
            through_on(k).wait_send()

    for copy in (*halo(0), *halo(1)):
        copy.wait_send()
    edges.wait_send()
    pl.when(in_run_high)(lambda: radial(0, (j, r)).wait_send())
    pl.when(seam_high)(lambda: seam_turned.wait_send())
    pl.when(has_low)(lambda: radial(1, (j, r)).wait_send())
    for d in range(1, n_chip):
        tile_copy(d).wait_send()
    exchange.wait_send()


def body(vorticity, rotor_field, courant, load_tiles, tile_block, tile_count):
    shape = vorticity.shape
    _, rows_az, rows_rad, cells_ax = shape
    slots, width = load_tiles.shape[2:]
    n_ra = lax.axis_size("ra")
    n_chip = n_ra // 2
    group = slots // n_chip

    def relay(n):
        return pltpu.VMEM((3, n, rows_rad, cells_ax), jnp.bfloat16)

    dma = pltpu.SemaphoreType.DMA
    around, through = len(AROUND), len(THROUGH)
    scratch = [
        pltpu.VMEM(shape, jnp.float32),
        pltpu.VMEM(shape, jnp.bfloat16),
        pltpu.VMEM(shape, jnp.bfloat16),
        pltpu.VMEM(shape, jnp.bfloat16),
        pltpu.VMEM((3, rows_az + 2, rows_rad, cells_ax), jnp.float32),
        pltpu.VMEM(shape, jnp.float32),
        pltpu.VMEM((2, 3, rows_rad, cells_ax), jnp.int16),
        pltpu.VMEM((2, 3, rows_rad, cells_ax), jnp.int16),
        pltpu.VMEM((2, rows_rad, TS), jnp.float32),
        pltpu.VMEM((2, rows_rad, TS), jnp.float32),
        relay(around),
        relay(around),
        relay(through),
        pltpu.VMEM((3, 2 * rows_az, cells_ax), jnp.float32),
        pltpu.VMEM((3, 2 * rows_az, cells_ax), jnp.bfloat16),
        pltpu.VMEM((3, 2 * rows_az, cells_ax), jnp.bfloat16),
        pltpu.VMEM((2, 3, rows_az, cells_ax), jnp.float32),
        pltpu.VMEM((2, 3, rows_az, cells_ax), jnp.float32),
        pltpu.VMEM((3, rows_az, cells_ax), jnp.float32),
        pltpu.VMEM((3, 2 * rows_az, cells_ax), jnp.bfloat16),
        pltpu.VMEM((slots, width), jnp.float32),
        pltpu.VMEM((1, slots), jnp.int32),
        pltpu.VMEM((1, n_ra), jnp.int32),
        pltpu.VMEM((slots, width + slots), jnp.float32),
        pltpu.VMEM((n_chip, group, width + slots), jnp.float32),
        pltpu.VMEM((n_chip, group, width + slots), jnp.float32),
        pltpu.VMEM((4 * slots, width), jnp.bfloat16),
        dma((6,)),
        dma((rows_az,)),
        dma((rows_az,)),
        dma((around,)),
        dma((around,)),
        dma((around,)),
        dma((around,)),
        dma((around,)),
        dma((through,)),
        dma((through,)),
        dma((5,)),
        dma((5,)),
        dma((4,)),
        dma((4,)),
        dma((n_chip,)),
        dma((n_chip,)),
        pltpu.SemaphoreType.REGULAR,
        pltpu.SemaphoreType.REGULAR,
        pltpu.SemaphoreType.REGULAR,
        pltpu.SemaphoreType.REGULAR,
        pltpu.SemaphoreType.REGULAR,
    ]
    return pl.pallas_call(
        kernel,
        name="step",
        out_shape=pltpu.VMEM(shape, jnp.float32),
        in_specs=[pl.BlockSpec(memory_space=pltpu.HBM)] * 6,
        out_specs=pl.BlockSpec(memory_space=pltpu.VMEM),
        scratch_shapes=scratch,
        compiler_params=pltpu.CompilerParams(
            collective_id=0, has_side_effects=True, vmem_limit_bytes=62 * 1024 * 1024
        ),
    )(vorticity, rotor_field, courant, load_tiles, tile_block, tile_count)


def solution(mesh):
    in_specs = (
        P(None, "azi", "ra", None),
        P(None, "azi", "ra", None),
        P(None, "azi", "ra", None),
        P("azi", "ra", None, None),
        P("azi", "ra", None),
        P("azi", "ra", None),
    )
    out_specs = P(None, "azi", "ra", None)
    return jax.shard_map(body, mesh=mesh, in_specs=in_specs, out_specs=out_specs, check_vma=False)
```

```python
import functools

import jax
import jax.numpy as jnp
from jax import lax
from jax.experimental import pallas as pl
from jax.experimental.pallas import tpu as pltpu
from jax.sharding import PartitionSpec as P

TS = 128
DIFFUSION = 0.15
MESH = pl.DeviceIdType.MESH
SOURCE_AFTER = (0, 1, 2, 7)
LEVELS = 32767.0
SMALLEST = 1e-30
CHIP_X = 4

AROUND = (3, 4, 5)
AROUND_LAST = 5
THROUGH = (0, 1, 2)
STRAIGHT = (0, 7, 5, 1, 2, 6)


def kernel(
    vort, rotor, cour, tiles, tile_id, tile_n, out,
    vbuf, cbuf, rbuf, rin, comb, src, code_out, code_in, scale_out, scale_in,
    relay_a, relay_b, relay_p, edge_f, edge_s, edge_r, edge_out, edge_in, seam_v, seam_s, seam_r,
    tbuf, idbuf, cntbuf, sbuf, trecv, tsib, tmat,
    lsem, r_send, r_recv, a_send, a_recv, b_send, b_recv, c_send,
    p_recv, q_send, h_send, h_recv, e_send, e_recv, t_send, t_recv, up_sem, down_sem, above_sem, seam_sem, seam_next,
):
    n_azi, n_ra = lax.axis_size("azi"), lax.axis_size("ra")
    n_y = n_azi // CHIP_X
    n_chip = n_ra // 2
    n_z = n_chip // 2
    rows_az, rows_rad, cells_ax = vbuf.shape[1:]
    j, r = lax.axis_index("azi"), lax.axis_index("ra")
    x, y = j % CHIP_X, j // CHIP_X
    chip, core = r // 2, r % 2
    z = chip % n_z
    first, last = x == 0, x == CHIP_X - 1
    has_low, has_high = r > 0, r < n_ra - 1
    z_low, z_high = z > 0, z < n_z - 1
    near_low = jnp.logical_and(core == 0, z_low)
    near_high = jnp.logical_and(core == 1, z_high)
    seam_low = jnp.logical_and(jnp.logical_and(core == 0, z == 0), has_low)
    seam_high = jnp.logical_and(jnp.logical_and(core == 1, z == n_z - 1), has_high)

    def at(xx, yy):
        return ((yy % n_y) * CHIP_X + xx % CHIP_X, r)

    following = ((j + 1) % n_azi, r)
    preceding = ((j + n_azi - 1) % n_azi, r)
    up_x, down_x = at(x + 1, y), at(x + 3, y)
    up_y, down_y = at(x, y + 1), at(x, y + n_y - 1)
    sibling = (j, chip * 2 + 1 - core)
    above, below = (j, r + 2), (j, r - 2)
    lower, higher = (j, r - 1), (j, r + 1)

    def local(ref, dst, k):
        return pltpu.make_async_copy(ref, dst, lsem.at[k])

    def row(ref, k):
        return ref.at[:, pl.ds(k, 1)]

    bar = pltpu.get_barrier_semaphore()

    def greet(device):
        pl.semaphore_signal(bar, inc=1, device_id=device, device_id_type=MESH)

    greet(following)
    greet(preceding)
    greet(sibling)
    greet((j, (r + n_ra // 2) % n_ra))
    pl.when(last)(lambda: greet(up_x))
    pl.when(first)(lambda: greet(down_x))
    pl.when(x == 2)(lambda: greet(at(1, y + 1)))
    pl.when(x == 1)(lambda: greet(at(2, y + n_y - 1)))
    pl.when(x == 1)(lambda: greet(at(0, y + 1)))

    @pl.when(first)
    def _():
        greet(up_y)
        greet(down_y)
        greet(at(1, y + n_y - 1))

    pl.when(z_high)(lambda: greet(above))
    pl.when(near_high)(lambda: greet(higher))
    others = 5 + 3 * first.astype(jnp.int32) + (x == 1).astype(jnp.int32)
    for near in (z_low, near_low):
        others = others + near.astype(jnp.int32)

    loads = [
        local(rotor, rbuf, 0),
        local(vort, vbuf, 1),
        local(tiles.at[0, 0], tbuf, 2),
        local(tile_id.at[0], idbuf, 3),
        local(tile_n.at[0], cntbuf, 4),
        local(cour, cbuf, 5),
    ]
    for load in loads:
        load.start()

    pl.semaphore_wait(bar, others)

    def remote(source, target, send, recv, device):
        return pltpu.make_async_remote_copy(
            src_ref=source, dst_ref=target, send_sem=send, recv_sem=recv,
            device_id=device, device_id_type=MESH,
        )

    def straight(k):
        return remote(row(rotor, k), row(rin, k), r_send.at[k], r_recv.at[k], following)

    def through(k):
        i = THROUGH.index(k)
        return remote(row(rotor, k), row(relay_p, i), r_send.at[k], p_recv.at[i], up_x)

    def through_on(k):
        i = THROUGH.index(k)
        return remote(row(relay_p, i), row(rin, k), q_send.at[i], r_recv.at[k], up_y)

    def around(k):
        i = AROUND.index(k)
        return remote(row(rotor, k), row(relay_a, i), a_send.at[i], a_recv.at[i], down_x)

    def around_on(k, device):
        i = AROUND.index(k)
        return remote(row(relay_a, i), row(relay_b, i), b_send.at[i], b_recv.at[i], device)

    def around_end(k, device):
        i = AROUND.index(k)
        return remote(row(relay_b, i), row(rin, k), c_send.at[i], r_recv.at[k], device)

    def halo(side):
        to = (preceding, following)[side]
        return (
            remote(code_out.at[side], code_in.at[side], h_send.at[side], h_recv.at[side], to),
            remote(
                scale_out.at[side], scale_in.at[side], h_send.at[3 + side], h_recv.at[3 + side], to
            ),
        )

    def encode(side, values):
        scale_lane = lax.broadcasted_iota(jnp.int32, (rows_rad, TS), 1)
        scales = jnp.zeros((rows_rad, TS), jnp.float32)
        for c in range(3):
            value = values(c)
            largest = jnp.max(jnp.abs(value), axis=1, keepdims=True)
            largest = jnp.maximum(largest, SMALLEST)
            code = jnp.round(value * (LEVELS / largest))
            code_out[side, c] = code.astype(jnp.int32).astype(jnp.int16)
            scales = jnp.where(scale_lane == c, largest * (1.0 / LEVELS), scales)
        scale_out[side] = scales
        for copy in halo(side):
            copy.start()

    def decode(side, c):
        return code_in[side, c].astype(jnp.int32).astype(jnp.float32) * scale_in[side, :, c : c + 1]

    edges = remote(edge_s, edge_r, h_send.at[2], h_recv.at[2], following)

    def radial(side, device):
        return remote(
            edge_out.at[side], edge_in.at[side], e_send.at[side], e_recv.at[side], device
        )

    seam_own = remote(edge_out.at[0], seam_v, e_send.at[2], e_recv.at[2], higher)
    seam_turned = remote(seam_s, seam_r, e_send.at[3], e_recv.at[3], ((j + 1) % n_azi, r + 1))

    capacity = tbuf.shape[0] // n_ra
    group = 2 * capacity

    def tile_copy(d):
        to = (chip + d) % n_chip
        return remote(
            sbuf.at[pl.ds(pl.multiple_of(to * group, group), group)], trecv.at[chip],
            t_send.at[d], t_recv.at[d], (j, to * 2 + core),
        )

    exchange = remote(trecv, tsib, t_send.at[0], t_recv.at[0], sibling)

    def start_row(k):
        if k in THROUGH or k == AROUND_LAST:
            other_way = around if k == AROUND_LAST else through
            pl.when(last)(lambda: other_way(k).start())
            pl.when(jnp.logical_not(last))(lambda: straight(k).start())
        else:
            straight(k).start()

    start_row(0)
    start_row(7)
    around(3).start()
    start_row(5)
    around(4).start()

    pl.when(z_low)(
        lambda: pl.semaphore_signal(above_sem, inc=1, device_id=below, device_id_type=MESH)
    )
    pl.when(z_low)(lambda: pl.semaphore_wait(up_sem, 1))

    @pl.when(z_high)
    def _():
        pl.semaphore_wait(above_sem, 1)
        pl.semaphore_signal(up_sem, inc=1, device_id=above, device_id_type=MESH)

    @pl.when(jnp.logical_not(z_high))
    def _():
        for d in range(1, n_z):
            pl.semaphore_signal(down_sem, inc=1, device_id=(j, r - 2 * d), device_id_type=MESH)

    top = jnp.logical_and(core == 1, z == n_z - 1)
    tell = jnp.logical_and(top, chip >= n_z)
    pl.when(tell)(
        lambda: pl.semaphore_signal(
            seam_sem, inc=1, device_id=(j, r - n_ra // 2), device_id_type=MESH
        )
    )

    loads[2].wait()
    loads[3].wait()
    loads[4].wait()
    slots = tbuf.shape[0]
    slot = lax.broadcasted_iota(jnp.int32, (slots, slots), 0)
    lane = lax.broadcasted_iota(jnp.int32, (slots, slots), 1)
    ids = jnp.broadcast_to(idbuf[...].astype(jnp.float32), (slots, slots))
    id_col = jnp.sum(jnp.where(slot == lane, ids, 0.0), axis=1, keepdims=True)
    slot_n = lax.broadcasted_iota(jnp.int32, (slots, n_ra), 0)
    lane_n = lax.broadcasted_iota(jnp.int32, (slots, n_ra), 1)
    counts = jnp.broadcast_to(cntbuf[...].astype(jnp.float32), (slots, n_ra))
    count_col = jnp.sum(
        jnp.where(slot_n // capacity == lane_n, counts, 0.0), axis=1, keepdims=True
    )
    used = (slot % capacity).astype(jnp.float32) < count_col
    width = tbuf.shape[1]
    sbuf[:, :width] = tbuf[...]
    sbuf[:, width:] = jnp.where(used, id_col, -1.0)
    trecv[pl.ds(chip, 1)] = sbuf[pl.ds(pl.multiple_of(chip * group, group), group)][None]

    def send_tiles(low_z, high_z):
        @pl.when(jnp.logical_and(z >= low_z, z <= high_z))
        def _():
            pl.when(z_high)(lambda: pl.semaphore_wait(down_sem, 1))
            for d in range(1, n_chip):
                tile_copy(d).start()

    send_tiles(n_z - 2, n_z - 1)

    @pl.when(seam_high)
    def _():
        pl.semaphore_wait(seam_sem, 1)
        pl.semaphore_signal(seam_next, inc=1, device_id=preceding, device_id_type=MESH)

    loads[0].wait()
    for c in range(3):
        for k in range(rows_az):
            whole = rbuf[c, k].astype(jnp.float32)
            edge_f[c, k : k + 1] = whole[:1]
            edge_f[c, rows_az + k : rows_az + k + 1] = whole[rows_rad - 1 :]
    edge_s[...] = edge_f[...].astype(jnp.bfloat16)
    @pl.when(seam_high)
    def _():
        high = [edge_f[c, rows_az:] for c in range(3)]
        seam_s[...] = jnp.concatenate([*high, high[0]], axis=0).astype(jnp.bfloat16)
        pl.semaphore_wait(seam_next, 1)
        seam_turned.start()

    edges.start()
    loads[1].wait()
    for c in range(3):
        for k in range(rows_az):
            edge_out[1, c, k : k + 1] = vbuf[c, k, :1]
            edge_out[0, c, k : k + 1] = vbuf[c, k, rows_rad - 1 :]

    pl.when(seam_high)(lambda: seam_own.start())
    start_row(1)
    encode(0, lambda c: vbuf[c, 0])
    start_row(2)
    start_row(6)

    def take(k):
        straight(k).wait_recv()
        for c in range(3):
            comb[c, k + 1] = vbuf[c, k] + rin[c, k].astype(jnp.float32)

    def relay_through(k):
        @pl.when(first)
        def _():
            through(k).wait_recv()
            through_on(k).start()

    def relay_first(k):
        around(k).wait_recv()
        if k == AROUND_LAST:
            around_on(k, down_x).start()
        else:
            pl.when(x == 2)(lambda: around_on(k, at(1, y + 1)).start())
            pl.when(x != 2)(lambda: around_on(k, down_x).start())

    def relay_second(k):
        around_on(k, down_x).wait_recv()
        around_end(k, at(0, y + 1) if k == AROUND_LAST else down_x).start()

    in_run_low = jnp.logical_and(has_low, jnp.logical_not(seam_low))
    in_run_high = jnp.logical_and(has_high, jnp.logical_not(seam_high))

    @pl.when(jnp.logical_not(in_run_low))
    def _():
        edge_in[0] = jnp.zeros_like(edge_in[0])

    @pl.when(jnp.logical_not(has_high))
    def _():
        edge_in[1] = jnp.zeros_like(edge_in[1])

    send_tiles(n_z - 4, n_z - 3)
    relay_through(0)
    relay_first(3)
    take(7)
    encode(1, lambda c: comb[c, rows_az])
    send_tiles(2, n_z - 5)
    relay_through(1)
    pl.when(x == 2)(lambda: relay_first(5))
    relay_first(4)
    relay_through(2)
    send_tiles(0, 1)
    edges.wait_recv()
    pl.when(seam_high)(lambda: seam_own.wait_send())
    for c in range(3):
        arrived = edge_r[c].astype(jnp.float32)
        edge_out[1, c] += arrived[:rows_az]
        edge_out[0, c] += arrived[rows_az:]
    pl.when(in_run_high)(lambda: radial(0, higher).start())
    pl.when(in_run_low)(lambda: radial(1, lower).start())
    relay_second(3)
    pl.when(x == 1)(lambda: relay_second(5))
    relay_second(4)
    take(0)
    take(1)

    @pl.when(seam_low)
    def _():
        tile_copy(1).wait_recv()
        radial(1, lower).start()

    pl.when(jnp.logical_not(seam_low))(lambda: tile_copy(1).wait_recv())
    for d in range(2, n_chip):
        tile_copy(d).wait_recv()
    exchange.start()

    axial = lax.broadcasted_iota(jnp.int32, (rows_rad, cells_ax), 1)
    radial_row = lax.broadcasted_iota(jnp.int32, (rows_rad, cells_ax), 0)
    position = (r * rows_rad + radial_row).astype(jnp.float32)
    inverse = 1.0 / (0.5 + (position + 0.5) / (rows_rad * n_ra))
    inverse_sq = inverse * inverse

    def stencil(k, with_source):
        v0 = cbuf[0, k].astype(jnp.float32)
        v1 = cbuf[1, k].astype(jnp.float32)
        v2 = cbuf[2, k].astype(jnp.float32)
        rad = (0.25 * DIFFUSION) * inverse - 0.5 * v0
        azi_even = DIFFUSION * inverse_sq
        azi_odd = 0.5 * v1 * inverse
        axi = 0.5 * v2
        middle = (1.0 - 4.0 * DIFFUSION) - (2.0 * DIFFUSION) * inverse_sq
        turn = (0.5 * DIFFUSION) * inverse_sq
        for c in range(3):
            f = comb[c, k + 1]
            nxt, prv = comb[c, k + 2], comb[c, k]
            up = pltpu.roll(f, rows_rad - 1, 0)
            up = jnp.where(radial_row == rows_rad - 1, edge_in[1, c, k : k + 1], up)
            down = pltpu.roll(f, 1, 0)
            down = jnp.where(radial_row == 0, edge_in[0, c, k : k + 1], down)
            right = jnp.where(axial == cells_ax - 1, 0.0, pltpu.roll(f, cells_ax - 1, 1))
            left = jnp.where(axial == 0, 0.0, pltpu.roll(f, 1, 1))
            total = middle * f
            if with_source:
                total = total + src[c, k]
            total = total + DIFFUSION * ((up + down) + (right + left))
            total = total + rad * (up - down) - axi * (right - left)
            total = total + azi_even * (nxt + prv) - azi_odd * (nxt - prv)
            if c == 0:
                total = total - (0.5 * turn) * f - turn * (comb[1, k + 2] - comb[1, k])
            elif c == 1:
                total = total - (0.5 * turn) * f + turn * (comb[0, k + 2] - comb[0, k])
            out[c, k] = total

    loads[5].wait()
    take(3)
    pl.when(in_run_low)(lambda: radial(0, (j, r)).wait_recv())
    pl.when(has_high)(lambda: radial(1, (j, r)).wait_recv())
    take(2)
    stencil(1, False)
    stencil(2, False)
    for copy in (*halo(0), *halo(1)):
        copy.wait_recv()
    for c in range(3):
        comb[c, rows_az + 1] = decode(0, c) + rbuf[c, 0].astype(jnp.float32)
        comb[c, 0] = decode(1, c)
    stencil(0, False)
    take(6)
    stencil(7, False)

    exchange.wait_recv()
    keep = (slot % group) // capacity == core
    halves = []
    for i, got in enumerate((trecv, tsib)):
        part = got[...].reshape(slots, width + slots)
        value = part[:, :width]
        top = value.astype(jnp.bfloat16)
        tmat[i * slots : (i + 1) * slots] = top
        tmat[(2 + i) * slots : (3 + i) * slots] = (value - top.astype(jnp.float32)).astype(
            jnp.bfloat16
        )
        halves.append(jnp.where(keep, part[:, width:], -1.0).T)
    blocks = jnp.concatenate(halves, axis=1)
    m = lax.broadcasted_iota(jnp.int32, blocks.shape, 0)
    per_row = cells_ax // TS
    local_block = (m % rows_rad) * per_row + m // rows_rad
    for a in range(rows_az):
        wanted = (local_block + a * rows_rad * per_row).astype(jnp.float32)
        hot = jnp.where(blocks == wanted, 1.0, 0.0).astype(jnp.bfloat16)
        placed = jnp.dot(
            jnp.concatenate([hot, hot], axis=1), tmat[...], preferred_element_type=jnp.float32
        )
        for b in range(per_row):
            for c in range(3):
                block = placed[b * rows_rad : (b + 1) * rows_rad, c * TS : (c + 1) * TS]
                if a in SOURCE_AFTER:
                    out[c, a, :, b * TS : (b + 1) * TS] += block
                else:
                    src[c, a, :, b * TS : (b + 1) * TS] = block

    take(5)
    stencil(6, True)
    take(4)
    stencil(3, True)
    stencil(4, True)
    stencil(5, True)

    @pl.when(seam_low)
    def _():
        seam_own.wait_recv()
        seam_turned.wait_recv()
        edge_inverse = inverse[:1]
        turned = seam_r[...].astype(jnp.float32)
        for c in range(3):
            arrived = seam_v[c] + turned[c * rows_az : (c + 1) * rows_az]
            for k in range(rows_az):
                v0 = cbuf[0, k].astype(jnp.float32)[:1]
                weight = DIFFUSION - (0.25 * DIFFUSION) * edge_inverse + 0.5 * v0
                out[c, k, :1] += weight * arrived[k : k + 1]

    for k in STRAIGHT:
        if k != AROUND_LAST:
            straight(k).wait_send()
    for k in AROUND:
        if k != AROUND_LAST:
            around(k).wait_send()
            around_on(k, down_x).wait_send()
            around_end(k, down_x).wait_send()
    pl.when(last)(lambda: around(AROUND_LAST).wait_send())
    pl.when(jnp.logical_not(last))(lambda: straight(AROUND_LAST).wait_send())
    pl.when(x == 2)(lambda: around_on(AROUND_LAST, down_x).wait_send())
    pl.when(x == 1)(lambda: around_end(AROUND_LAST, down_x).wait_send())

    @pl.when(first)
    def _():
        for k in THROUGH:
            through_on(k).wait_send()

    for copy in (*halo(0), *halo(1)):
        copy.wait_send()
    edges.wait_send()
    pl.when(in_run_high)(lambda: radial(0, (j, r)).wait_send())
    pl.when(seam_high)(lambda: seam_turned.wait_send())
    pl.when(has_low)(lambda: radial(1, (j, r)).wait_send())
    for d in range(1, n_chip):
        tile_copy(d).wait_send()
    exchange.wait_send()


def body(vorticity, rotor_field, courant, load_tiles, tile_block, tile_count):
    shape = vorticity.shape
    _, rows_az, rows_rad, cells_ax = shape
    slots, width = load_tiles.shape[2:]
    n_ra = lax.axis_size("ra")
    n_chip = n_ra // 2
    group = slots // n_chip

    def relay(n):
        return pltpu.VMEM((3, n, rows_rad, cells_ax), jnp.bfloat16)

    dma = pltpu.SemaphoreType.DMA
    around, through = len(AROUND), len(THROUGH)
    scratch = [
        pltpu.VMEM(shape, jnp.float32),
        pltpu.VMEM(shape, jnp.bfloat16),
        pltpu.VMEM(shape, jnp.bfloat16),
        pltpu.VMEM(shape, jnp.bfloat16),
        pltpu.VMEM((3, rows_az + 2, rows_rad, cells_ax), jnp.float32),
        pltpu.VMEM(shape, jnp.float32),
        pltpu.VMEM((2, 3, rows_rad, cells_ax), jnp.int16),
        pltpu.VMEM((2, 3, rows_rad, cells_ax), jnp.int16),
        pltpu.VMEM((2, rows_rad, TS), jnp.float32),
        pltpu.VMEM((2, rows_rad, TS), jnp.float32),
        relay(around),
        relay(around),
        relay(through),
        pltpu.VMEM((3, 2 * rows_az, cells_ax), jnp.float32),
        pltpu.VMEM((3, 2 * rows_az, cells_ax), jnp.bfloat16),
        pltpu.VMEM((3, 2 * rows_az, cells_ax), jnp.bfloat16),
        pltpu.VMEM((2, 3, rows_az, cells_ax), jnp.float32),
        pltpu.VMEM((2, 3, rows_az, cells_ax), jnp.float32),
        pltpu.VMEM((3, rows_az, cells_ax), jnp.float32),
        pltpu.VMEM((4 * rows_az, cells_ax), jnp.bfloat16),
        pltpu.VMEM((4 * rows_az, cells_ax), jnp.bfloat16),
        pltpu.VMEM((slots, width), jnp.float32),
        pltpu.VMEM((1, slots), jnp.int32),
        pltpu.VMEM((1, n_ra), jnp.int32),
        pltpu.VMEM((slots, width + slots), jnp.float32),
        pltpu.VMEM((n_chip, group, width + slots), jnp.float32),
        pltpu.VMEM((n_chip, group, width + slots), jnp.float32),
        pltpu.VMEM((4 * slots, width), jnp.bfloat16),
        dma((6,)),
        dma((rows_az,)),
        dma((rows_az,)),
        dma((around,)),
        dma((around,)),
        dma((around,)),
        dma((around,)),
        dma((around,)),
        dma((through,)),
        dma((through,)),
        dma((5,)),
        dma((5,)),
        dma((4,)),
        dma((4,)),
        dma((n_chip,)),
        dma((n_chip,)),
        pltpu.SemaphoreType.REGULAR,
        pltpu.SemaphoreType.REGULAR,
        pltpu.SemaphoreType.REGULAR,
        pltpu.SemaphoreType.REGULAR,
        pltpu.SemaphoreType.REGULAR,
    ]
    return pl.pallas_call(
        kernel,
        name="step",
        out_shape=pltpu.VMEM(shape, jnp.float32),
        in_specs=[pl.BlockSpec(memory_space=pltpu.HBM)] * 6,
        out_specs=pl.BlockSpec(memory_space=pltpu.VMEM),
        scratch_shapes=scratch,
        compiler_params=pltpu.CompilerParams(
            collective_id=0, has_side_effects=True, vmem_limit_bytes=62 * 1024 * 1024
        ),
    )(vorticity, rotor_field, courant, load_tiles, tile_block, tile_count)


def solution(mesh):
    in_specs = (
        P(None, "azi", "ra", None),
        P(None, "azi", "ra", None),
        P(None, "azi", "ra", None),
        P("azi", "ra", None, None),
        P("azi", "ra", None),
        P("azi", "ra", None),
    )
    out_specs = P(None, "azi", "ra", None)
    return jax.shard_map(body, mesh=mesh, in_specs=in_specs, out_specs=out_specs, check_vma=False)
```
